256 devices in a mesh: outer: 16 (over z, core), shard: 16 (over x, y).
Axes of the slice: x: 4, y: 4, z: 8, core: 2. Of those that a mesh axis runs over, the one named last changes fastest.
Arguments:
- base: float32 [5120, 1024], P('shard'), may hold values from -16 to 16
- local: bfloat16 [16, 5120, 1024], P('outer', 'shard'), may hold values from -28 to 28
- error: float32 [16, 5120, 1024], P('outer', 'shard'), may hold values from -4 to 4
- momentum: float32 [5120, 1024], P('shard'), may hold values from -4 to 4
- query: float32 [1024, 64], replicated, may hold values from -6 to 6
Outputs:
- new_base: float32 [5120, 1024], P('shard')
- new_error: float32 [16, 5120, 1024], P('outer', 'shard')
- new_momentum: float32 [5120, 1024], P('shard')
The draws below stay inside these ranges and needn't reach their ends.
All inputs are finite; a program needn't handle non-finite values.
Results may differ from the reference program's by a relative error of at most 0.0003.
Values sent between devices are 32-bit elements; how exact they have to be, the bound alone decides.
No kernel may reach another device: no remote copies, remote signals or barrier semaphores. Data moves between devices by JAX's collectives and lax.ppermute only.
A program may use at most 64 MiB of HBM per device.

```python
import math
import jax
import jax.numpy as jnp
from jax import lax

D = 5120
KV = 1024
RANK = 64
ITERS = 2
REPLICAS = 16


def scale_lines(key):
    row_key = jax.random.fold_in(key, 11)
    col_key = jax.random.fold_in(key, 12)
    rising = jnp.exp(math.log(3.0) * jnp.arange(D, dtype=jnp.float32) / D)
    rows = jnp.exp(jax.random.uniform(row_key, (D, 1), jnp.float32, -1.15, 0.0)) * rising[:, None]
    cols = jnp.exp(jax.random.uniform(col_key, (1, KV), jnp.float32, -1.15, 0.0))
    return (rows, cols)


def rough_field(key, shape):
    drawn = jnp.clip(jax.random.normal(jax.random.fold_in(key, 1), shape, jnp.float32), -5.0, 5.0)
    return drawn


def base_field(key):
    rows, cols = scale_lines(key)
    return rough_field(jax.random.fold_in(key, 13), (D, KV)) * rows * cols


def draw_base(key, part):
    return base_field(key)


def draw_local(key, part):
    shared = base_field(key)
    rows, cols = scale_lines(key)
    key = jax.random.fold_in(key, 5)
    common = rough_field(jax.random.fold_in(key, 21), (D, KV))
    noise = rough_field(jax.random.fold_in(key, 22), (REPLICAS, D, KV))
    delta = 0.5 * (common[None] + 0.6 * noise) * rows[None] * cols[None]
    return (shared[None] - delta).astype(jnp.bfloat16)


def level_of(stream_key, shape, pieces, least, top_value):
    loudness, own = 1.0, jax.random.fold_in(stream_key, 6)
    for axis_at, shards_of in pieces:
        steps = jnp.exp(jax.random.uniform(jax.random.fold_in(own, axis_at), (shards_of,), jnp.float32, least / len(pieces), top_value / len(pieces)))
        loudness = loudness * jnp.repeat(steps, shape[axis_at] // shards_of).reshape([-1 if axis == axis_at else 1 for axis in range(len(shape))])
    return loudness


def normal_values(key, shape, scale, bound, shards=(), held_as=jnp.bfloat16):
    entries = jax.random.normal(key, shape, jnp.float32) * scale
    if len(shards) > 0:
        entries = level_of(key, shape, shards, -0.22, 0.18) * entries
    return jnp.clip(entries, min=-bound, max=bound).astype(held_as)


def setup_inputs(seed: int = 0) -> dict:
    splits = jax.random.split(jax.random.key(seed), 6)
    base = draw_base(jax.random.fold_in(splits[5], 71), 0)
    local = draw_local(jax.random.fold_in(splits[5], 71), 0)
    error = normal_values(splits[2], (REPLICAS, D, KV), 0.5, 4.0, ((0, 16), (1, 16)), jnp.float32)
    momentum = normal_values(splits[3], (D, KV), 0.5, 4.0, ((0, 16),), jnp.float32)
    query = normal_values(splits[4], (KV, RANK), 1.0, 6.0, (), jnp.float32)
    return dict(base=base, local=local, error=error, momentum=momentum, query=query)


momentum_decay = 0.9
outer_rate = 0.7

def orthonormal(left):
    gram = jnp.dot(left.T, left, precision=lax.Precision.HIGHEST)
    factor = jnp.linalg.cholesky(gram)
    return lax.linalg.triangular_solve(factor, left, left_side=False, lower=True, transpose_a=True)

def reference(base, local, error, momentum, query):
    field = base[None] - local.astype(jnp.float32) + error
    right = query
    basis = None
    for step in range(ITERS):
        left = jnp.einsum('rdk,kq->dq', field, right, precision=lax.Precision.HIGHEST) / REPLICAS
        basis = orthonormal(left)
        right = jnp.einsum('rdk,dq->kq', field, basis, precision=lax.Precision.HIGHEST) / REPLICAS
    approx = jnp.dot(basis, right.T, precision=lax.Precision.HIGHEST)
    new_error = field - approx[None]
    new_momentum = momentum_decay * momentum + approx
    new_base = base - outer_rate * (approx + momentum_decay * new_momentum)
    return (new_base, new_error, new_momentum)
```

```python
import jax
import jax.numpy as jnp
from jax import lax
from jax.sharding import Mesh, PartitionSpec as P

ITERS = 2
REPLICAS = 16
RANK = 64
NZ, NC, NX, NY = 8, 2, 4, 4
HALF = 160
KV = 1024
SLICE = KV // NZ

momentum_decay = 0.9
outer_rate = 0.7

HI = lax.Precision.HIGHEST
SWAP = [(0, 1), (1, 0)]


def gathered(chunk, axes, n):
    return lax.all_to_all(jnp.broadcast_to(chunk[None], (n,) + chunk.shape), axes, 0, 0, tiled=True)


def reduced_right(piece, left, z, c):
    wt = lax.dot_general(left, piece, (((0,), (0,)), ((), ())), precision=HI)
    gram = lax.dot_general(left, left, (((0,), (0,)), ((), ())), precision=HI)
    rows = lax.dynamic_slice_in_dim(gram, z * 8, 8, 0).reshape(2, 4, RANK)
    rows = jnp.pad(rows, ((0, 0), (0, 4), (0, 128 - RANK)))
    pack = jnp.concatenate([wt.reshape(2, 32, 128), rows], axis=1)
    mine = lax.dynamic_index_in_dim(pack, c, 0, keepdims=False)
    other = lax.dynamic_index_in_dim(pack, 1 - c, 0, keepdims=False)
    chunk = mine + lax.ppermute(other, "c", SWAP)
    chunk = gathered(chunk, ("x", "y"), NX * NY).sum(0)
    full = gathered(chunk, ("z", "c"), NZ * NC).reshape(NZ, NC, 40, 128)
    wt = full[:, :, :32].transpose(1, 2, 0, 3).reshape(RANK, KV)
    gram = full[:, :, 32:36, :RANK].reshape(RANK, RANK)
    return wt, gram


def inverse_factor(gram):
    factor = jnp.linalg.cholesky(gram)
    return lax.linalg.triangular_solve(
        factor, jnp.eye(RANK, dtype=jnp.float32), left_side=True, lower=True
    )


def body(base, local, error, momentum, query):
    z, c = lax.axis_index("z"), lax.axis_index("c")
    field = base - local[0].astype(jnp.float32) + error[0]
    halves = field.reshape(2, HALF, KV)
    mine = lax.dynamic_index_in_dim(halves, c, 0, keepdims=False)
    other = lax.dynamic_index_in_dim(halves, 1 - c, 0, keepdims=False)
    pair = mine + lax.ppermute(other, "c", SWAP)
    left_part = jnp.dot(pair, query, precision=HI)
    left_pack = jnp.concatenate([left_part[:80], left_part[80:]], axis=1)
    send = jnp.concatenate(
        [
            pair.reshape(HALF, NZ, SLICE).transpose(1, 0, 2),
            jnp.broadcast_to(left_pack[None], (NZ, 80, 128)),
        ],
        axis=1,
    )
    got = lax.all_to_all(send, "z", 0, 0, tiled=True).sum(0) / REPLICAS
    piece = got[:HALF]
    left = jnp.concatenate([got[HALF:, :RANK], got[HALF:, RANK:]], axis=0)
    rows = lax.all_gather(piece, "z")
    wt, gram = reduced_right(piece, left, z, c)
    for step in range(1, ITERS):
        inv = inverse_factor(gram)
        rt = jnp.dot(inv, wt, precision=HI)
        left = jnp.einsum("zdk,qzk->dq", rows, rt.reshape(RANK, NZ, SLICE), precision=HI)
        wt, gram = reduced_right(piece, left, z, c)
    inv = inverse_factor(gram)
    theirs = lax.ppermute(left, "c", SWAP)
    left = jnp.where(c == 0, jnp.concatenate([left, theirs], 0), jnp.concatenate([theirs, left], 0))
    basis = lax.dot_general(left, inv, (((1,), (1,)), ((), ())), precision=HI)
    rt = jnp.dot(inv, wt, precision=HI)
    approx = jnp.dot(basis, rt, precision=HI)
    new_error = (field - approx)[None]
    new_momentum = momentum_decay * momentum + approx
    new_base = base - outer_rate * (approx + momentum_decay * new_momentum)
    return (new_base, new_error, new_momentum)


def solution(mesh):
    mesh = Mesh(mesh.devices.reshape(NZ, NC, NX, NY), ("z", "c", "x", "y"))
    outer, shard = ("z", "c"), ("x", "y")
    in_specs = (
        P(shard, None),
        P(outer, shard, None),
        P(outer, shard, None),
        P(shard, None),
        P(),
    )
    out_specs = (P(shard, None), P(outer, shard, None), P(shard, None))
    return jax.shard_map(body, mesh=mesh, in_specs=in_specs, out_specs=out_specs, check_vma=False)
```

```python
import functools
import jax
import jax.numpy as jnp
from jax import lax
from jax.experimental import pallas as pl
from jax.experimental.pallas import tpu as pltpu
from jax.sharding import Mesh, PartitionSpec as P

ITERS = 2
REPLICAS = 16
RANK = 64
NZ, NC, NX, NY = 8, 2, 4, 4
ROWS = 320
HALF = 160
KV = 1024
SLICE = KV // NZ
PACK = 40

momentum_decay = 0.9
outer_rate = 0.7

HI = lax.Precision.HIGHEST
SWAP = [(0, 1), (1, 0)]
F32 = jnp.float32
VMEM = pl.BlockSpec(memory_space=pltpu.VMEM)
SMEM = pl.BlockSpec(memory_space=pltpu.SMEM)
ANY = pl.BlockSpec(memory_space=pl.ANY)
PARAMS = pltpu.CompilerParams(vmem_limit_bytes=32 * 2**20)


def shape(*dims):
    return jax.ShapeDtypeStruct(dims, F32)


def dot(a, b, ca, cb):
    return lax.dot_general(a, b, (((ca,), (cb,)), ((), ())), precision=HI, preferred_element_type=F32)


def spread(x):
    return jnp.broadcast_to(x, (8, 128))


def inverse_factor(gram):
    n = RANK // 8
    eye = (
        lax.broadcasted_iota(jnp.int32, (RANK, RANK), 0)
        == lax.broadcasted_iota(jnp.int32, (RANK, RANK), 1)
    ).astype(F32)
    full = jnp.concatenate([gram, eye], axis=1)
    a = [full[8 * i : 8 * i + 8] for i in range(n)]
    sub = lax.broadcasted_iota(jnp.int32, (8, 128), 0)
    for b in range(n):
        p = a[b]
        at = 8 * b
        e = [spread(p[:, at + j : at + j + 1]) for j in range(8)]
        cols = [[spread(a[i][:, at + j : at + j + 1]) for j in range(8)] for i in range(b + 1, n)]
        for k in range(8):
            s = lax.rsqrt(spread(e[k][k : k + 1]))
            f = jnp.where(sub > k, e[k] * (s * s), 0.0)
            u = [None] * 8
            for j in range(k + 1, 8):
                row = spread(e[j][k : k + 1])
                u[j] = row * s
                e[j] = e[j] - f * row
            prow = spread(p[k : k + 1])
            p = jnp.where(sub == k, prow * s, p - f * prow)
            for ci in cols:
                ci[k] = ci[k] * s
                for j in range(k + 1, 8):
                    ci[j] = ci[j] - ci[k] * u[j]
        for i in range(b + 1, n):
            for k in range(8):
                a[i] = a[i] - cols[i - b - 1][k] * spread(p[k : k + 1])
        a[b] = p
    return jnp.concatenate(a, axis=0)[:, RANK:]


def unpack(full):
    wt = jnp.concatenate(
        [jnp.concatenate([full[z, c, :32] for c in range(NC)], axis=0) for z in range(NZ)], axis=1
    )
    gram = jnp.concatenate(
        [full[z, c, 32:36, :RANK] for z in range(NZ) for c in range(NC)], axis=0
    )
    return wt, gram


def put_message(left, piece, z, c, gram_ref, pack_ref, keep_ref, send_ref):
    wt = dot(left, piece, 0, 0)
    gram_ref[...] = jnp.zeros((RANK, 128), F32)
    gram_ref[:, :RANK] = dot(left, left, 0, 0)
    rows = gram_ref[pl.ds(pl.multiple_of(z * 8, 8), 8), :]
    pack_ref[0, :32] = wt[:32]
    pack_ref[1, :32] = wt[32:]
    pack_ref[0, 32:] = rows
    pack_ref[1, 32:] = jnp.concatenate([rows[4:], rows[:4]], axis=0)
    keep_ref[...] = pack_ref[c]
    send_ref[...] = pack_ref[1 - c]


def first_send(mine_ref, theirs_ref, query_ref, out_ref):
    pair = mine_ref[...] + theirs_ref[...]
    left = dot(pair, query_ref[...], 1, 0)
    packed = jnp.concatenate([left[: HALF // 2], left[HALF // 2 :]], axis=1)
    for z in range(NZ):
        out_ref[z, :HALF] = pair[:, z * SLICE : (z + 1) * SLICE]
        out_ref[z, HALF:] = packed


def first_left(at_ref, got_ref, piece_ref, keep_ref, send_ref, gram_ref, pack_ref):
    total = got_ref[0]
    for z in range(1, NZ):
        total = total + got_ref[z]
    total = total * (1.0 / REPLICAS)
    piece = total[:HALF]
    piece_ref[...] = piece
    left = jnp.concatenate([total[HALF:, :RANK], total[HALF:, RANK:]], axis=0)
    put_message(left, piece, at_ref[0], at_ref[1], gram_ref, pack_ref, keep_ref, send_ref)


def sum_spread(*refs):
    *ins, out_ref = refs
    parts = []
    for ref in ins:
        parts += [ref[...]] if len(ref.shape) == 2 else [ref[i] for i in range(ref.shape[0])]
    total = functools.reduce(lambda a, b: a + b, parts)
    for i in range(out_ref.shape[0]):
        out_ref[i] = total


def next_left(at_ref, full_ref, rows_ref, piece_ref, left_ref, keep_ref, send_ref, gram_ref, pack_ref):
    wt, gram = unpack(full_ref)
    rt = dot(inverse_factor(gram), wt, 1, 0)
    rows = jnp.concatenate([rows_ref[z] for z in range(NZ)], axis=1)
    left = dot(rows, rt, 1, 1)
    left_ref[...] = left
    put_message(left, piece_ref[...], at_ref[0], at_ref[1], gram_ref, pack_ref, keep_ref, send_ref)


def finish(at_ref, full_ref, mine_ref, theirs_ref, field_in, base_in, mom_in, base_out, err_out, mom_out,
           left_ref, field, base, mom, nbase, nerr, nmom, in_sem, out_sem):
    loads = [
        pltpu.make_async_copy(src, dst, in_sem.at[i])
        for i, (src, dst) in enumerate([(field_in, field), (base_in, base), (mom_in, mom)])
    ]
    for load in loads:
        load.start()
    c = at_ref[1]
    left_ref[c] = mine_ref[...]
    left_ref[1 - c] = theirs_ref[...]
    wt, gram = unpack(full_ref)
    inv = inverse_factor(gram)
    rt = dot(inv, wt, 1, 0)
    stores = []
    for load in loads:
        load.wait()
    part = HALF // 2
    for i in range(ROWS // part):
        here = pl.ds(i * part, part)
        basis = dot(left_ref[i // 2, pl.ds((i % 2) * part, part)], inv, 1, 1)
        approx = dot(basis, rt, 1, 0)
        nerr[here] = field[here] - approx
        momentum = momentum_decay * mom[here] + approx
        nmom[here] = momentum
        nbase[here] = base[here] - outer_rate * (approx + momentum_decay * momentum)
        for j, (src, dst) in enumerate([(nbase, base_out), (nerr, err_out), (nmom, mom_out)]):
            store = pltpu.make_async_copy(src.at[here], dst.at[here], out_sem.at[j, i])
            store.start()
            stores.append(store)
    for store in stores:
        store.wait()


def gathered(operand, axes):
    return lax.all_to_all(operand, axes, 0, 0, tiled=True)


def summed_right(keep, send):
    xy, zc = NX * NY, NZ * NC
    theirs = lax.ppermute(send, "c", SWAP)
    chunks = pl.pallas_call(
        sum_spread, out_shape=shape(xy, PACK, 128), in_specs=[VMEM] * 2, out_specs=VMEM
    )(keep, theirs)
    got = gathered(chunks, ("x", "y"))
    chunks = pl.pallas_call(
        sum_spread, out_shape=shape(zc, PACK, 128), in_specs=[VMEM], out_specs=VMEM
    )(got)
    return gathered(chunks, ("z", "c")).reshape(NZ, NC, PACK, 128)


def body(base, local, error, momentum, query):
    z, c = lax.axis_index("z"), lax.axis_index("c")
    at = jnp.stack([z, c]).astype(jnp.int32)
    field = base - local[0].astype(F32) + error[0]
    halves = field.reshape(2, HALF, KV)
    mine = lax.dynamic_index_in_dim(halves, c, 0, keepdims=False)
    other = lax.dynamic_index_in_dim(halves, 1 - c, 0, keepdims=False)
    theirs = lax.ppermute(other, "c", SWAP)
    send = pl.pallas_call(
        first_send,
        out_shape=shape(NZ, HALF + HALF // 2, 128),
        in_specs=[VMEM] * 3,
        out_specs=VMEM,
        compiler_params=PARAMS,
    )(mine, theirs, query)
    got = lax.all_to_all(send, "z", 0, 0, tiled=True)
    message = [shape(PACK, 128), shape(PACK, 128)]
    scratch = [pltpu.VMEM((RANK, 128), F32), pltpu.VMEM((2, PACK, 128), F32)]
    piece, keep, send = pl.pallas_call(
        first_left,
        out_shape=[shape(HALF, SLICE)] + message,
        in_specs=[SMEM, VMEM],
        out_specs=[VMEM] * 3,
        scratch_shapes=scratch,
        compiler_params=PARAMS,
    )(at, got)
    rows = gathered(jnp.broadcast_to(piece[None], (NZ, HALF, SLICE)), "z")
    full = summed_right(keep, send)
    for step in range(1, ITERS):
        left, keep, send = pl.pallas_call(
            next_left,
            out_shape=[shape(HALF, RANK)] + message,
            in_specs=[SMEM] + [VMEM] * 3,
            out_specs=[VMEM] * 3,
            scratch_shapes=scratch,
            compiler_params=PARAMS,
        )(at, full, rows, piece)
        theirs = lax.ppermute(left, "c", SWAP)
        full = summed_right(keep, send)
    big = pltpu.VMEM((ROWS, KV), F32)
    new_base, new_error, new_momentum = pl.pallas_call(
        finish,
        out_shape=[shape(ROWS, KV)] * 3,
        in_specs=[SMEM] + [VMEM] * 3 + [ANY] * 3,
        out_specs=[ANY] * 3,
        scratch_shapes=[pltpu.VMEM((2, HALF, RANK), F32)]
        + [big] * 6
        + [pltpu.SemaphoreType.DMA((3,)), pltpu.SemaphoreType.DMA((3, 4))],
        compiler_params=PARAMS,
    )(at, full, left, theirs, field, base, momentum)
    return new_base, new_error[None], new_momentum


def solution(mesh):
    mesh = Mesh(mesh.devices.reshape(NZ, NC, NX, NY), ("z", "c", "x", "y"))
    outer, shard = ("z", "c"), ("x", "y")
    in_specs = (
        P(shard, None),
        P(outer, shard, None),
        P(outer, shard, None),
        P(shard, None),
        P(),
    )
    out_specs = (P(shard, None), P(outer, shard, None), P(shard, None))
    return jax.shard_map(body, mesh=mesh, in_specs=in_specs, out_specs=out_specs, check_vma=False)
```

```python
import functools
import jax
import jax.numpy as jnp
from jax import lax
from jax.experimental import pallas as pl
from jax.experimental.pallas import tpu as pltpu
from jax.sharding import Mesh, PartitionSpec as P

ITERS = 2
REPLICAS = 16
RANK = 64
NZ, NC, NX, NY = 8, 2, 4, 4
XY, ZC = NX * NY, NZ * NC
ROWS = 320
HALF = ROWS // 2
KV = 1024
SLICE = KV // NZ
PART = RANK // NC
LEFT = ROWS * PART // 128
GRAM = PART * RANK // 128
PACK = PART + GRAM

momentum_decay = 0.9
outer_rate = 0.7

HI = lax.Precision.HIGHEST
SWAP = [(0, 1), (1, 0)]
F32 = jnp.float32
VMEM = pl.BlockSpec(memory_space=pltpu.VMEM)
SMEM = pl.BlockSpec(memory_space=pltpu.SMEM)
ANY = pl.BlockSpec(memory_space=pl.ANY)


def shape(*dims):
    return jax.ShapeDtypeStruct(dims, F32)


def call(kernel, outs, ins, scratch=(), mib=8, flops=10**6):
    return pl.pallas_call(
        kernel,
        out_shape=outs,
        in_specs=ins,
        out_specs=jax.tree.map(lambda _: VMEM, outs),
        scratch_shapes=list(scratch),
        compiler_params=pltpu.CompilerParams(vmem_limit_bytes=mib * 2**20),
        cost_estimate=pl.CostEstimate(flops=flops, bytes_accessed=2**20, transcendentals=0),
    )


def dot(a, b, ca, cb):
    return lax.dot_general(a, b, (((ca,), (cb,)), ((), ())), precision=HI, preferred_element_type=F32)


def add_up(ref):
    return functools.reduce(lambda a, b: a + b, [ref[i] for i in range(ref.shape[0])])


def spread(x):
    return jnp.broadcast_to(x, (8, 128))


def inverse_factor(gram):
    n = RANK // 8
    eye = (
        lax.broadcasted_iota(jnp.int32, (RANK, RANK), 0)
        == lax.broadcasted_iota(jnp.int32, (RANK, RANK), 1)
    ).astype(F32)
    full = jnp.concatenate([gram, eye], axis=1)
    a = [full[8 * i : 8 * i + 8] for i in range(n)]
    sub = lax.broadcasted_iota(jnp.int32, (8, 128), 0)
    for b in range(n):
        p = a[b]
        at = 8 * b
        e = [spread(p[:, at + j : at + j + 1]) for j in range(8)]
        cols = [[spread(a[i][:, at + j : at + j + 1]) for j in range(8)] for i in range(b + 1, n)]
        for k in range(8):
            s = lax.rsqrt(spread(e[k][k : k + 1]))
            f = jnp.where(sub > k, e[k] * (s * s), 0.0)
            u = [None] * 8
            for j in range(k + 1, 8):
                row = spread(e[j][k : k + 1])
                u[j] = row * s
                e[j] = e[j] - f * row
            prow = spread(p[k : k + 1])
            p = jnp.where(sub == k, prow * s, p - f * prow)
            for ci in cols:
                ci[k] = ci[k] * s
                for j in range(k + 1, 8):
                    ci[j] = ci[j] - ci[k] * u[j]
        for i in range(b + 1, n):
            for k in range(8):
                a[i] = a[i] - cols[i - b - 1][k] * spread(p[k : k + 1])
        a[b] = p
    return jnp.concatenate(a, axis=0)[:, RANK:]


def in_order(c, mine, theirs):
    first = c == 0
    return jnp.where(first, mine, theirs), jnp.where(first, theirs, mine)


def gram_of(c, mine, theirs):
    halves = in_order(c, mine, theirs)
    return jnp.concatenate([p for h in halves for p in (h[:, :RANK], h[:, RANK:])], axis=0)


def put_message(c, left_ref, piece, out_ref):
    own = left_ref[pl.ds(pl.multiple_of(c * PART, PART), PART)]
    wt = dot(own, piece, 1, 0)
    gram = dot(own, left_ref[...], 1, 1)
    gram = jnp.concatenate([gram[:GRAM], gram[GRAM:]], axis=1)
    for i in range(XY):
        out_ref[i, :PART] = wt
        out_ref[i, PART:] = gram


def first_send(at_ref, field_ref, theirs_ref, query_ref, out_ref):
    mine = field_ref[pl.ds(pl.multiple_of(at_ref[0] * HALF, HALF), HALF)]
    pair = mine + theirs_ref[...]
    left = dot(pair, query_ref[...], 1, 0)
    packed = jnp.concatenate([left[: HALF // 2], left[HALF // 2 :]], axis=1)
    for z in range(NZ):
        out_ref[z, :HALF] = pair[:, z * SLICE : (z + 1) * SLICE]
        out_ref[z, HALF:] = packed


def mean_over_z(got_ref, out_ref):
    out_ref[...] = add_up(got_ref) * (1.0 / REPLICAS)


def first_message(at_ref, mine_ref, theirs_ref, out_ref, piece_ref, left_ref):
    c = at_ref[0]
    halves = in_order(c, mine_ref[...], theirs_ref[...])
    piece = jnp.concatenate([h[:HALF] for h in halves], axis=0)
    left = jnp.concatenate([p for h in halves for p in (h[HALF:, :RANK], h[HALF:, RANK:])], axis=0)
    piece_ref[...] = piece
    left_ref[...] = left.T
    put_message(c, left_ref, piece, out_ref)


def left_parts(got_ref, piece_ref, out_ref, gram_ref):
    total = add_up(got_ref)
    gram_ref[...] = total[PART:]
    left = dot(piece_ref[...], total[:PART], 1, 1)
    packed = jnp.concatenate([left[i * LEFT : (i + 1) * LEFT] for i in range(128 // PART)], axis=1)
    for z in range(NZ):
        out_ref[z] = packed


def factor(at_ref, mine_ref, theirs_ref, out_ref):
    out_ref[...] = inverse_factor(gram_of(at_ref[0], mine_ref[...], theirs_ref[...]))


def total_of(got_ref, out_ref):
    out_ref[...] = add_up(got_ref)


def next_message(at_ref, mine_ref, theirs_ref, inv_ref, piece_ref, out_ref, left_ref):
    c = at_ref[0]
    first, second = in_order(c, mine_ref[...], theirs_ref[...])
    left = jnp.concatenate(
        [
            jnp.concatenate([h[:, i * PART : (i + 1) * PART] for h in (first, second)], axis=1)
            for i in range(128 // PART)
        ],
        axis=0,
    )
    left_ref[...] = dot(inv_ref[...], left, 1, 1)
    put_message(c, left_ref, piece_ref[...], out_ref)


def right_parts(got_ref, out_ref, gram_ref):
    total = add_up(got_ref)
    gram_ref[...] = total[PART:]
    for i in range(ZC):
        out_ref[i] = total[:PART]


def coefficients(at_ref, mine_ref, theirs_ref, left_ref, out_ref):
    inv = inverse_factor(gram_of(at_ref[0], mine_ref[...], theirs_ref[...]))
    basis = dot(inv, left_ref[...], 1, 0)
    out_ref[...] = dot(basis, inv, 0, 0)


def finish(full_ref, coef_ref, field_in, base_in, mom_in, base_out, err_out, mom_out,
           field, base, mom, nbase, nerr, nmom, in_sem, out_sem):
    loads = [
        pltpu.make_async_copy(src, dst, in_sem.at[i])
        for i, (src, dst) in enumerate([(field_in, field), (base_in, base), (mom_in, mom)])
    ]
    for load in loads:
        load.start()
    wt = jnp.concatenate(
        [jnp.concatenate([full_ref[z * NC + c] for c in range(NC)], axis=0) for z in range(NZ)], axis=1
    )
    for load in loads:
        load.wait()
    stores = []
    part = HALF // 2
    for i in range(ROWS // part):
        here = pl.ds(i * part, part)
        approx = dot(coef_ref[here], wt, 1, 0)
        nerr[here] = field[here] - approx
        momentum = momentum_decay * mom[here] + approx
        nmom[here] = momentum
        nbase[here] = base[here] - outer_rate * (approx + momentum_decay * momentum)
        for j, (src, dst) in enumerate([(nbase, base_out), (nerr, err_out), (nmom, mom_out)]):
            store = pltpu.make_async_copy(src.at[here], dst.at[here], out_sem.at[j, i])
            store.start()
            stores.append(store)
    for store in stores:
        store.wait()


def exchange(operand, axes):
    return lax.all_to_all(operand, axes, 0, 0, tiled=True)


def swap(x):
    return lax.ppermute(x, "c", SWAP)


def body(base, local, error, momentum, query):
    c = lax.axis_index("c")
    at = c.astype(jnp.int32)[None]
    there = (1 - c) * HALF
    rows = lambda x: lax.dynamic_slice_in_dim(x, there, HALF, 0)
    theirs = swap(rows(base) - rows(local[0]).astype(F32) + rows(error[0]))
    field = base - local[0].astype(F32) + error[0]
    send = call(first_send, shape(NZ, HALF + HALF // 2, 128), [SMEM] + [VMEM] * 3)(
        at, field, theirs, query
    )
    mean = call(mean_over_z, shape(HALF + HALF // 2, 128), [VMEM])(exchange(send, "z"))
    send, piece, left = call(
        first_message, [shape(XY, PACK, 128), shape(ROWS, SLICE), shape(RANK, ROWS)], [SMEM] + [VMEM] * 2
    )(at, mean, swap(mean))
    for step in range(1, ITERS):
        send, gram = call(left_parts, [shape(NZ, LEFT, 128), shape(GRAM, 128)], [VMEM] * 2)(
            exchange(send, ("x", "y")), piece
        )
        got = exchange(send, "z")
        inv = call(factor, shape(RANK, RANK), [SMEM] + [VMEM] * 2, flops=10**9)(at, gram, swap(gram))
        part = call(total_of, shape(LEFT, 128), [VMEM])(got)
        send, left = call(
            next_message, [shape(XY, PACK, 128), shape(RANK, ROWS)], [SMEM] + [VMEM] * 4
        )(at, part, swap(part), inv, piece)
    send, gram = call(right_parts, [shape(ZC, PART, 128), shape(GRAM, 128)], [VMEM])(
        exchange(send, ("x", "y"))
    )
    full = exchange(send, ("z", "c"))
    coef = call(coefficients, shape(ROWS, RANK), [SMEM] + [VMEM] * 3, flops=10**9)(
        at, gram, swap(gram), left
    )
    big = pltpu.VMEM((ROWS, KV), F32)
    new_base, new_error, new_momentum = pl.pallas_call(
        finish,
        out_shape=[shape(ROWS, KV)] * 3,
        in_specs=[VMEM] * 2 + [ANY] * 3,
        out_specs=[ANY] * 3,
        scratch_shapes=[big] * 6
        + [pltpu.SemaphoreType.DMA((3,)), pltpu.SemaphoreType.DMA((3, 4))],
        compiler_params=pltpu.CompilerParams(vmem_limit_bytes=16 * 2**20),
    )(full, coef, field, base, momentum)
    return new_base, new_error[None], new_momentum


def solution(mesh):
    mesh = Mesh(mesh.devices.reshape(NZ, NC, NX, NY), ("z", "c", "x", "y"))
    outer, shard = ("z", "c"), ("x", "y")
    in_specs = (
        P(shard, None),
        P(outer, shard, None),
        P(outer, shard, None),
        P(shard, None),
        P(),
    )
    out_specs = (P(shard, None), P(outer, shard, None), P(shard, None))
    return jax.shard_map(body, mesh=mesh, in_specs=in_specs, out_specs=out_specs, check_vma=False)
```

```python
import functools
import jax
import jax.numpy as jnp
from jax import lax
from jax.experimental import pallas as pl
from jax.experimental.pallas import tpu as pltpu
from jax.sharding import Mesh, PartitionSpec as P

ITERS = 2
REPLICAS = 16
RANK = 64
NZ, NC, NX, NY = 8, 2, 4, 4
XY, ZC = NX * NY, NZ * NC
ROWS = 320
HALF = ROWS // 2
KV = 1024
SLICE = KV // NZ
PART = RANK // NC
LEFT = ROWS * PART // 128
GRAM = PART * RANK // 128
PACK = PART + GRAM

momentum_decay = 0.9
outer_rate = 0.7

HI = lax.Precision.HIGHEST
SWAP = [(0, 1), (1, 0)]
F32 = jnp.float32
VMEM = pl.BlockSpec(memory_space=pltpu.VMEM)
SMEM = pl.BlockSpec(memory_space=pltpu.SMEM)
HBM = pl.BlockSpec(memory_space=pltpu.HBM)


def shape(*dims):
    return jax.ShapeDtypeStruct(dims, F32)


def call(kernel, outs, ins, scratch=(), mib=8, flops=10**6):
    return pl.pallas_call(
        kernel,
        out_shape=outs,
        in_specs=ins,
        out_specs=jax.tree.map(lambda _: VMEM, outs),
        scratch_shapes=list(scratch),
        compiler_params=pltpu.CompilerParams(vmem_limit_bytes=mib * 2**20),
        cost_estimate=pl.CostEstimate(flops=flops, bytes_accessed=2**20, transcendentals=0),
    )


def dot(a, b, ca, cb):
    return lax.dot_general(a, b, (((ca,), (cb,)), ((), ())), precision=HI, preferred_element_type=F32)


def add_up(ref):
    return functools.reduce(lambda a, b: a + b, [ref[i] for i in range(ref.shape[0])])


def spread(x):
    return jnp.broadcast_to(x, (8, 128))


def inverse_factor(gram):
    n = RANK // 8
    eye = (
        lax.broadcasted_iota(jnp.int32, (RANK, RANK), 0)
        == lax.broadcasted_iota(jnp.int32, (RANK, RANK), 1)
    ).astype(F32)
    full = jnp.concatenate([gram, eye], axis=1)
    a = [full[8 * i : 8 * i + 8] for i in range(n)]
    sub = lax.broadcasted_iota(jnp.int32, (8, 128), 0)
    for b in range(n):
        p = a[b]
        at = 8 * b
        e = [spread(p[:, at + j : at + j + 1]) for j in range(8)]
        cols = [[spread(a[i][:, at + j : at + j + 1]) for j in range(8)] for i in range(b + 1, n)]
        for k in range(8):
            s = lax.rsqrt(spread(e[k][k : k + 1]))
            f = jnp.where(sub > k, e[k] * (s * s), 0.0)
            u = [None] * 8
            for j in range(k + 1, 8):
                row = spread(e[j][k : k + 1])
                u[j] = row * s
                e[j] = e[j] - f * row
            prow = spread(p[k : k + 1])
            p = jnp.where(sub == k, prow * s, p - f * prow)
            for ci in cols:
                ci[k] = ci[k] * s
                for j in range(k + 1, 8):
                    ci[j] = ci[j] - ci[k] * u[j]
        for i in range(b + 1, n):
            for k in range(8):
                a[i] = a[i] - cols[i - b - 1][k] * spread(p[k : k + 1])
        a[b] = p
    return jnp.concatenate(a, axis=0)[:, RANK:]


def in_order(c, mine, theirs):
    first = c == 0
    return jnp.where(first, mine, theirs), jnp.where(first, theirs, mine)


def gram_of(c, mine, theirs):
    halves = in_order(c, mine, theirs)
    return jnp.concatenate([p for h in halves for p in (h[:, :RANK], h[:, RANK:])], axis=0)


def put_message(c, left_ref, piece, out_ref):
    own = left_ref[pl.ds(pl.multiple_of(c * PART, PART), PART)]
    wt = dot(own, piece, 1, 0)
    gram = dot(own, left_ref[...], 1, 1)
    gram = jnp.concatenate([gram[:GRAM], gram[GRAM:]], axis=1)
    for i in range(XY):
        out_ref[i, :PART] = wt
        out_ref[i, PART:] = gram


def half_field(there, base_in, local_in, error_in, base, local, error, sem, out_ref):
    part = HALF // 2
    loads = []
    for i in range(2):
        here = pl.ds(i * part, part)
        rows = pl.ds(pl.multiple_of(there + i * part, part), part)
        for j, (src, dst) in enumerate([(base_in, base), (local_in.at[0], local), (error_in.at[0], error)]):
            load = pltpu.make_async_copy(src.at[rows], dst.at[here], sem.at[i, j])
            load.start()
            loads.append(load)
    for i in range(2):
        here = pl.ds(i * part, part)
        for load in loads[3 * i : 3 * i + 3]:
            load.wait()
        out_ref[here] = base[here] - local[here].astype(F32) + error[here]


def other_half(at_ref, base_in, local_in, error_in, out_ref, base, local, error, sem):
    half_field((1 - at_ref[0]) * HALF, base_in, local_in, error_in, base, local, error, sem, out_ref)


def own_half(at_ref, base_in, local_in, error_in, out_ref, base, local, error, sem):
    half_field(at_ref[0] * HALF, base_in, local_in, error_in, base, local, error, sem, out_ref)


def first_send(mine_ref, theirs_ref, query_ref, out_ref):
    pair = mine_ref[...] + theirs_ref[...]
    left = dot(pair, query_ref[...], 1, 1)
    packed = jnp.concatenate([left[: HALF // 2], left[HALF // 2 :]], axis=1)
    for z in range(NZ):
        out_ref[z, :HALF] = pair[:, z * SLICE : (z + 1) * SLICE]
        out_ref[z, HALF:] = packed


def mean_over_z(got_ref, out_ref):
    out_ref[...] = add_up(got_ref) * (1.0 / REPLICAS)


def first_message(at_ref, mine_ref, theirs_ref, out_ref, piece_ref, left_ref):
    c = at_ref[0]
    halves = in_order(c, mine_ref[...], theirs_ref[...])
    piece = jnp.concatenate([h[:HALF] for h in halves], axis=0)
    left = jnp.concatenate([p for h in halves for p in (h[HALF:, :RANK], h[HALF:, RANK:])], axis=0)
    piece_ref[...] = piece
    left_ref[...] = left.T
    put_message(c, left_ref, piece, out_ref)


def left_parts(got_ref, piece_ref, out_ref, gram_ref):
    total = add_up(got_ref)
    gram_ref[...] = total[PART:]
    left = dot(piece_ref[...], total[:PART], 1, 1)
    packed = jnp.concatenate([left[i * LEFT : (i + 1) * LEFT] for i in range(128 // PART)], axis=1)
    for z in range(NZ):
        out_ref[z] = packed


def factor(at_ref, mine_ref, theirs_ref, out_ref):
    out_ref[...] = inverse_factor(gram_of(at_ref[0], mine_ref[...], theirs_ref[...]))


def total_of(got_ref, inv_ref, out_ref):
    out_ref[...] = add_up(got_ref)


def next_message(at_ref, mine_ref, theirs_ref, inv_ref, piece_ref, out_ref, left_ref):
    c = at_ref[0]
    first, second = in_order(c, mine_ref[...], theirs_ref[...])
    left = jnp.concatenate(
        [
            jnp.concatenate([h[:, i * PART : (i + 1) * PART] for h in (first, second)], axis=1)
            for i in range(128 // PART)
        ],
        axis=0,
    )
    left_ref[...] = dot(inv_ref[...], left, 1, 1)
    put_message(c, left_ref, piece_ref[...], out_ref)


def right_parts(got_ref, out_ref, gram_ref):
    total = add_up(got_ref)
    gram_ref[...] = total[PART:]
    for i in range(ZC):
        out_ref[i] = total[:PART]


def coefficients(at_ref, mine_ref, theirs_ref, left_ref, own_ref, other_ref, base_in, mom_in,
                 coef_ref, field_ref, base_ref, mom_ref, sem):
    loads = [
        pltpu.make_async_copy(src, dst, sem.at[i])
        for i, (src, dst) in enumerate([(base_in, base_ref), (mom_in, mom_ref)])
    ]
    for load in loads:
        load.start()
    c = at_ref[0]
    inv = inverse_factor(gram_of(c, mine_ref[...], theirs_ref[...]))
    basis = dot(inv, left_ref[...], 1, 0)
    coef_ref[...] = dot(basis, inv, 0, 0)
    field_ref[pl.ds(pl.multiple_of(c * HALF, HALF), HALF)] = own_ref[...]
    field_ref[pl.ds(pl.multiple_of((1 - c) * HALF, HALF), HALF)] = other_ref[...]
    for load in loads:
        load.wait()


def finish(full_ref, coef_ref, field, base, mom, base_out, err_out, mom_out, nbase, nerr, nmom, out_sem):
    wt = jnp.concatenate(
        [jnp.concatenate([full_ref[z * NC + c] for c in range(NC)], axis=0) for z in range(NZ)], axis=1
    )
    stores = []
    part = HALF // 2
    for i in range(ROWS // part):
        here = pl.ds(i * part, part)
        approx = dot(coef_ref[here], wt, 1, 0)
        nerr[here] = field[here] - approx
        momentum = momentum_decay * mom[here] + approx
        nmom[here] = momentum
        nbase[here] = base[here] - outer_rate * (approx + momentum_decay * momentum)
        for j, (src, dst) in enumerate([(nbase, base_out), (nerr, err_out), (nmom, mom_out)]):
            store = pltpu.make_async_copy(src.at[here], dst.at[here], out_sem.at[j, i])
            store.start()
            stores.append(store)
    for store in stores:
        store.wait()


def exchange(operand, axes):
    return lax.all_to_all(operand, axes, 0, 0, tiled=True)


def swap(x):
    return lax.ppermute(x, "c", SWAP)


def body(base, local, error, momentum, query):
    c = lax.axis_index("c")
    at = c.astype(jnp.int32)[None]
    buffers = [pltpu.VMEM((HALF, KV), t) for t in (F32, jnp.bfloat16, F32)]
    buffers.append(pltpu.SemaphoreType.DMA((2, 3)))
    half = lambda kernel: call(kernel, shape(HALF, KV), [SMEM] + [HBM] * 3, buffers, mib=60)(
        at, base, local, error
    )
    other = half(other_half)
    theirs = swap(other)
    own = half(own_half)
    send = call(first_send, shape(NZ, HALF + HALF // 2, 128), [VMEM] * 3)(own, theirs, query.T)
    mean = call(mean_over_z, shape(HALF + HALF // 2, 128), [VMEM])(exchange(send, "z"))
    send, piece, left = call(
        first_message, [shape(XY, PACK, 128), shape(ROWS, SLICE), shape(RANK, ROWS)], [SMEM] + [VMEM] * 2
    )(at, mean, swap(mean))
    for step in range(1, ITERS):
        send, gram = call(left_parts, [shape(NZ, LEFT, 128), shape(GRAM, 128)], [VMEM] * 2)(
            exchange(send, ("x", "y")), piece
        )
        got = exchange(send, "z")
        inv = call(factor, shape(RANK, RANK), [SMEM] + [VMEM] * 2, flops=10**9)(at, gram, swap(gram))
        part = call(total_of, shape(LEFT, 128), [VMEM, HBM])(got, inv)
        send, left = call(
            next_message, [shape(XY, PACK, 128), shape(RANK, ROWS)], [SMEM] + [VMEM] * 4
        )(at, part, swap(part), inv, piece)
    send, gram = call(right_parts, [shape(ZC, PART, 128), shape(GRAM, 128)], [VMEM])(
        exchange(send, ("x", "y"))
    )
    full = exchange(send, ("z", "c"))
    whole = shape(ROWS, KV)
    coef, field, old_base, old_momentum = call(
        coefficients,
        [shape(ROWS, RANK)] + [whole] * 3,
        [SMEM] + [VMEM] * 5 + [HBM] * 2,
        [pltpu.SemaphoreType.DMA((2,))],
        mib=16,
        flops=10**9,
    )(at, gram, swap(gram), left, own, other, base, momentum)
    new_base, new_error, new_momentum = pl.pallas_call(
        finish,
        out_shape=[whole] * 3,
        in_specs=[VMEM] * 5,
        out_specs=[HBM] * 3,
        scratch_shapes=[pltpu.VMEM((ROWS, KV), F32)] * 3 + [pltpu.SemaphoreType.DMA((3, 4))],
        compiler_params=pltpu.CompilerParams(vmem_limit_bytes=16 * 2**20),
    )(full, coef, field, old_base, old_momentum)
    return new_base, new_error[None], new_momentum


def solution(mesh):
    mesh = Mesh(mesh.devices.reshape(NZ, NC, NX, NY), ("z", "c", "x", "y"))
    outer, shard = ("z", "c"), ("x", "y")
    in_specs = (
        P(shard, None),
        P(outer, shard, None),
        P(outer, shard, None),
        P(shard, None),
        P(),
    )
    out_specs = (P(shard, None), P(outer, shard, None), P(shard, None))
    return jax.shard_map(body, mesh=mesh, in_specs=in_specs, out_specs=out_specs, check_vma=False)
```

```python
import functools
import jax
import jax.numpy as jnp
from jax import lax
from jax.experimental import pallas as pl
from jax.experimental.pallas import tpu as pltpu
from jax.sharding import Mesh, PartitionSpec as P

ITERS = 2
REPLICAS = 16
RANK = 64
NZ, NC, NX, NY = 8, 2, 4, 4
XY, ZC = NX * NY, NZ * NC
ROWS = 320
HALF = ROWS // 2
KV = 1024
SLICE = KV // NZ
PART = RANK // NC
LEFT = ROWS * PART // 128
GRAM = PART * RANK // 128
PACK = PART + GRAM

momentum_decay = 0.9
outer_rate = 0.7

HI = lax.Precision.HIGHEST
SWAP = [(0, 1), (1, 0)]
F32 = jnp.float32
VMEM = pl.BlockSpec(memory_space=pltpu.VMEM)
SMEM = pl.BlockSpec(memory_space=pltpu.SMEM)
HBM = pl.BlockSpec(memory_space=pltpu.HBM)


def shape(*dims):
    return jax.ShapeDtypeStruct(dims, F32)


def call(kernel, outs, ins, scratch=(), mib=8, flops=10**6):
    return pl.pallas_call(
        kernel,
        out_shape=outs,
        in_specs=ins,
        out_specs=jax.tree.map(lambda _: VMEM, outs),
        scratch_shapes=list(scratch),
        compiler_params=pltpu.CompilerParams(vmem_limit_bytes=mib * 2**20),
        cost_estimate=pl.CostEstimate(flops=flops, bytes_accessed=2**20, transcendentals=0),
    )


def dot(a, b, ca, cb):
    return lax.dot_general(a, b, (((ca,), (cb,)), ((), ())), precision=HI, preferred_element_type=F32)


def add_up(ref):
    return functools.reduce(lambda a, b: a + b, [ref[i] for i in range(ref.shape[0])])


def spread(x):
    return jnp.broadcast_to(x, (8, 128))


def inverse_factor(gram):
    n = RANK // 8
    eye = (
        lax.broadcasted_iota(jnp.int32, (RANK, RANK), 0)
        == lax.broadcasted_iota(jnp.int32, (RANK, RANK), 1)
    ).astype(F32)
    full = jnp.concatenate([gram, eye], axis=1)
    a = [full[8 * i : 8 * i + 8] for i in range(n)]
    sub = lax.broadcasted_iota(jnp.int32, (8, 128), 0)
    for b in range(n):
        p = a[b]
        at = 8 * b
        e = [spread(p[:, at + j : at + j + 1]) for j in range(8)]
        cols = [[spread(a[i][:, at + j : at + j + 1]) for j in range(8)] for i in range(b + 1, n)]
        for k in range(8):
            s = lax.rsqrt(spread(e[k][k : k + 1]))
            f = jnp.where(sub > k, e[k] * (s * s), 0.0)
            u = [None] * 8
            for j in range(k + 1, 8):
                row = spread(e[j][k : k + 1])
                u[j] = row * s
                e[j] = e[j] - f * row
            prow = spread(p[k : k + 1])
            p = jnp.where(sub == k, prow * s, p - f * prow)
            for ci in cols:
                ci[k] = ci[k] * s
                for j in range(k + 1, 8):
                    ci[j] = ci[j] - ci[k] * u[j]
        for i in range(b + 1, n):
            for k in range(8):
                a[i] = a[i] - cols[i - b - 1][k] * spread(p[k : k + 1])
        a[b] = p
    return jnp.concatenate(a, axis=0)[:, RANK:]


def in_order(c, mine, theirs):
    first = c == 0
    return jnp.where(first, mine, theirs), jnp.where(first, theirs, mine)


def gram_of(c, mine, theirs):
    halves = in_order(c, mine, theirs)
    return jnp.concatenate([p for h in halves for p in (h[:, :RANK], h[:, RANK:])], axis=0)


def put_message(c, left_ref, piece, out_ref):
    own = left_ref[pl.ds(pl.multiple_of(c * PART, PART), PART)]
    wt = dot(own, piece, 1, 0)
    gram = dot(own, left_ref[...], 1, 1)
    gram = jnp.concatenate([gram[:GRAM], gram[GRAM:]], axis=1)
    for i in range(XY):
        out_ref[i, :PART] = wt
        out_ref[i, PART:] = gram


def half_field(there, base_in, local_in, error_in, base, local, error, sem, out_ref):
    part = HALF // 2
    loads = []
    for i in range(2):
        here = pl.ds(i * part, part)
        rows = pl.ds(pl.multiple_of(there + i * part, part), part)
        for j, (src, dst) in enumerate([(base_in, base), (local_in.at[0], local), (error_in.at[0], error)]):
            load = pltpu.make_async_copy(src.at[rows], dst.at[here], sem.at[i, j])
            load.start()
            loads.append(load)
    for i in range(2):
        here = pl.ds(i * part, part)
        for load in loads[3 * i : 3 * i + 3]:
            load.wait()
        out_ref[here] = base[here] - local[here].astype(F32) + error[here]


def other_half(at_ref, base_in, local_in, error_in, out_ref, base, local, error, sem):
    half_field((1 - at_ref[0]) * HALF, base_in, local_in, error_in, base, local, error, sem, out_ref)


def own_half(at_ref, base_in, local_in, error_in, out_ref, base, local, error, sem):
    half_field(at_ref[0] * HALF, base_in, local_in, error_in, base, local, error, sem, out_ref)


def first_send(mine_ref, theirs_ref, query_ref, out_ref):
    pair = mine_ref[...] + theirs_ref[...]
    left = dot(pair, query_ref[...], 1, 1)
    packed = jnp.concatenate([left[: HALF // 2], left[HALF // 2 :]], axis=1)
    for z in range(NZ):
        out_ref[z, :HALF] = pair[:, z * SLICE : (z + 1) * SLICE]
        out_ref[z, HALF:] = packed


def mean_over_z(got_ref, out_ref):
    out_ref[...] = add_up(got_ref) * (1.0 / REPLICAS)


def first_message(at_ref, mine_ref, theirs_ref, out_ref, piece_ref, left_ref):
    c = at_ref[0]
    halves = in_order(c, mine_ref[...], theirs_ref[...])
    piece = jnp.concatenate([h[:HALF] for h in halves], axis=0)
    left = jnp.concatenate([p for h in halves for p in (h[HALF:, :RANK], h[HALF:, RANK:])], axis=0)
    piece_ref[...] = piece
    left_ref[...] = left.T
    put_message(c, left_ref, piece, out_ref)


def left_parts(got_ref, piece_ref, out_ref, gram_ref):
    total = add_up(got_ref)
    gram_ref[...] = total[PART:]
    left = dot(piece_ref[...], total[:PART], 1, 1)
    packed = jnp.concatenate([left[i * LEFT : (i + 1) * LEFT] for i in range(128 // PART)], axis=1)
    for z in range(NZ):
        out_ref[z] = packed


def factor(at_ref, mine_ref, theirs_ref, out_ref):
    out_ref[...] = inverse_factor(gram_of(at_ref[0], mine_ref[...], theirs_ref[...]))


def total_of(got_ref, inv_ref, out_ref):
    out_ref[...] = add_up(got_ref)


def next_message(at_ref, mine_ref, theirs_ref, inv_ref, piece_ref, out_ref, left_ref):
    c = at_ref[0]
    first, second = in_order(c, mine_ref[...], theirs_ref[...])
    left = jnp.concatenate(
        [
            jnp.concatenate([h[:, i * PART : (i + 1) * PART] for h in (first, second)], axis=1)
            for i in range(128 // PART)
        ],
        axis=0,
    )
    left_ref[...] = dot(inv_ref[...], left, 1, 1)
    put_message(c, left_ref, piece_ref[...], out_ref)


def right_parts(got_ref, out_ref, gram_ref):
    total = add_up(got_ref)
    gram_ref[...] = total[PART:]
    for i in range(ZC):
        out_ref[i] = total[:PART]


def coefficients(at_ref, mine_ref, theirs_ref, left_ref, own_ref, other_ref, base_in, mom_in,
                 coef_ref, field_ref, base_ref, mom_ref, sem):
    loads = [
        pltpu.make_async_copy(src, dst, sem.at[i])
        for i, (src, dst) in enumerate([(base_in, base_ref), (mom_in, mom_ref)])
    ]
    for load in loads:
        load.start()
    c = at_ref[0]
    inv = inverse_factor(gram_of(c, mine_ref[...], theirs_ref[...]))
    basis = dot(inv, left_ref[...], 1, 0)
    coef_ref[...] = dot(basis, inv, 0, 0)
    field_ref[pl.ds(pl.multiple_of(c * HALF, HALF), HALF)] = own_ref[...]
    field_ref[pl.ds(pl.multiple_of((1 - c) * HALF, HALF), HALF)] = other_ref[...]
    for load in loads:
        load.wait()


def finish(full_ref, coef_ref, field, base, mom, base_out, err_out, mom_out, nbase, nerr, nmom, out_sem):
    wt = jnp.concatenate(
        [jnp.concatenate([full_ref[z * NC + c] for c in range(NC)], axis=0) for z in range(NZ)], axis=1
    )
    stores = []
    part = HALF // 2
    for i in range(ROWS // part):
        here = pl.ds(i * part, part)
        approx = dot(coef_ref[here], wt, 1, 0)
        nerr[here] = field[here] - approx
        momentum = momentum_decay * mom[here] + approx
        nmom[here] = momentum
        nbase[here] = base[here] - outer_rate * (approx + momentum_decay * momentum)
        for j, (src, dst) in enumerate([(nbase, base_out), (nerr, err_out), (nmom, mom_out)]):
            store = pltpu.make_async_copy(src.at[here], dst.at[here], out_sem.at[j, i])
            store.start()
            stores.append(store)
    for store in stores:
        store.wait()


def exchange(operand, axes):
    return lax.all_to_all(operand, axes, 0, 0, tiled=True)


def in_hbm(x):
    return pltpu.with_memory_space_constraint(x, pltpu.HBM)


def in_vmem(x):
    return pltpu.with_memory_space_constraint(x, pltpu.VMEM)


def swap(x):
    return lax.ppermute(x, "c", SWAP)


def body(base, local, error, momentum, query):
    c = lax.axis_index("c")
    at = c.astype(jnp.int32)[None]
    buffers = [pltpu.VMEM((HALF, KV), t) for t in (F32, jnp.bfloat16, F32)]
    buffers.append(pltpu.SemaphoreType.DMA((2, 3)))
    half = lambda kernel: call(kernel, shape(HALF, KV), [SMEM] + [HBM] * 3, buffers)(
        at, in_hbm(base), in_hbm(local), in_hbm(error)
    )
    other = half(other_half)
    theirs = swap(other)
    own = half(own_half)
    send = call(first_send, shape(NZ, HALF + HALF // 2, 128), [VMEM] * 3)(own, theirs, query.T)
    mean = call(mean_over_z, shape(HALF + HALF // 2, 128), [VMEM])(exchange(send, "z"))
    send, piece, left = call(
        first_message, [shape(XY, PACK, 128), shape(ROWS, SLICE), shape(RANK, ROWS)], [SMEM] + [VMEM] * 2
    )(at, mean, swap(mean))
    for step in range(1, ITERS):
        send, gram = call(left_parts, [shape(NZ, LEFT, 128), shape(GRAM, 128)], [VMEM] * 2)(
            exchange(send, ("x", "y")), piece
        )
        got = exchange(send, "z")
        inv = call(factor, shape(RANK, RANK), [SMEM] + [VMEM] * 2, flops=10**9)(at, gram, swap(gram))
        part = call(total_of, shape(LEFT, 128), [VMEM, HBM])(got, inv)
        send, left = call(
            next_message, [shape(XY, PACK, 128), shape(RANK, ROWS)], [SMEM] + [VMEM] * 4
        )(at, part, swap(part), inv, piece)
    send, gram = call(right_parts, [shape(ZC, PART, 128), shape(GRAM, 128)], [VMEM])(
        exchange(send, ("x", "y"))
    )
    full = exchange(send, ("z", "c"))
    whole = shape(ROWS, KV)
    coef, field, old_base, old_momentum = call(
        coefficients,
        [shape(ROWS, RANK)] + [whole] * 3,
        [SMEM] + [VMEM] * 5 + [HBM] * 2,
        [pltpu.SemaphoreType.DMA((2,))],
        mib=16,
        flops=10**9,
    )(at, gram, swap(gram), left, own, other, in_hbm(base), in_hbm(momentum))
    new_base, new_error, new_momentum = pl.pallas_call(
        finish,
        out_shape=[whole] * 3,
        in_specs=[VMEM] * 5,
        out_specs=[HBM] * 3,
        scratch_shapes=[pltpu.VMEM((ROWS, KV), F32)] * 3 + [pltpu.SemaphoreType.DMA((3, 4))],
        compiler_params=pltpu.CompilerParams(vmem_limit_bytes=16 * 2**20),
    )(full, coef, in_vmem(field), in_vmem(old_base), in_vmem(old_momentum))
    return new_base, new_error[None], new_momentum


def solution(mesh):
    mesh = Mesh(mesh.devices.reshape(NZ, NC, NX, NY), ("z", "c", "x", "y"))
    outer, shard = ("z", "c"), ("x", "y")
    in_specs = (
        P(shard, None),
        P(outer, shard, None),
        P(outer, shard, None),
        P(shard, None),
        P(),
    )
    out_specs = (P(shard, None), P(outer, shard, None), P(shard, None))
    return jax.shard_map(body, mesh=mesh, in_specs=in_specs, out_specs=out_specs, check_vma=False)
```

```python
import functools
import jax
import jax.numpy as jnp
from jax import lax
from jax.experimental import pallas as pl
from jax.experimental.pallas import tpu as pltpu
from jax.sharding import Mesh, PartitionSpec as P

ITERS = 2
REPLICAS = 16
RANK = 64
NZ, NC, NX, NY = 8, 2, 4, 4
XY, ZC = NX * NY, NZ * NC
ROWS = 320
HALF = ROWS // 2
KV = 1024
SLICE = KV // NZ
PART = RANK // NC
LEFT = ROWS * PART // 128
GRAM = PART * RANK // 128
PACK = PART + GRAM

momentum_decay = 0.9
outer_rate = 0.7

HI = lax.Precision.HIGHEST
SWAP = [(0, 1), (1, 0)]
F32 = jnp.float32
VMEM = pl.BlockSpec(memory_space=pltpu.VMEM)
SMEM = pl.BlockSpec(memory_space=pltpu.SMEM)
HBM = pl.BlockSpec(memory_space=pltpu.HBM)


def shape(*dims):
    return jax.ShapeDtypeStruct(dims, F32)


def call(kernel, outs, ins, scratch=(), mib=8, flops=10**6):
    return pl.pallas_call(
        kernel,
        out_shape=outs,
        in_specs=ins,
        out_specs=jax.tree.map(lambda _: VMEM, outs),
        scratch_shapes=list(scratch),
        compiler_params=pltpu.CompilerParams(vmem_limit_bytes=mib * 2**20),
        cost_estimate=pl.CostEstimate(flops=flops, bytes_accessed=2**20, transcendentals=0),
    )


def dot(a, b, ca, cb):
    return lax.dot_general(a, b, (((ca,), (cb,)), ((), ())), precision=HI, preferred_element_type=F32)


def add_up(ref):
    return functools.reduce(lambda a, b: a + b, [ref[i] for i in range(ref.shape[0])])


def spread(x):
    return jnp.broadcast_to(x, (8, 128))


def inverse_factor(gram):
    n = RANK // 8
    eye = (
        lax.broadcasted_iota(jnp.int32, (RANK, RANK), 0)
        == lax.broadcasted_iota(jnp.int32, (RANK, RANK), 1)
    ).astype(F32)
    full = jnp.concatenate([gram, eye], axis=1)
    a = [full[8 * i : 8 * i + 8] for i in range(n)]
    sub = lax.broadcasted_iota(jnp.int32, (8, 128), 0)
    for b in range(n):
        p = a[b]
        at = 8 * b
        e = [spread(p[:, at + j : at + j + 1]) for j in range(8)]
        cols = [[spread(a[i][:, at + j : at + j + 1]) for j in range(8)] for i in range(b + 1, n)]
        for k in range(8):
            s = lax.rsqrt(spread(e[k][k : k + 1]))
            f = jnp.where(sub > k, e[k] * (s * s), 0.0)
            u = [None] * 8
            for j in range(k + 1, 8):
                row = spread(e[j][k : k + 1])
                u[j] = row * s
                e[j] = e[j] - f * row
            prow = spread(p[k : k + 1])
            p = jnp.where(sub == k, prow * s, p - f * prow)
            for ci in cols:
                ci[k] = ci[k] * s
                for j in range(k + 1, 8):
                    ci[j] = ci[j] - ci[k] * u[j]
        for i in range(b + 1, n):
            for k in range(8):
                a[i] = a[i] - cols[i - b - 1][k] * spread(p[k : k + 1])
        a[b] = p
    return jnp.concatenate(a, axis=0)[:, RANK:]


def in_order(c, mine, theirs):
    first = c == 0
    return jnp.where(first, mine, theirs), jnp.where(first, theirs, mine)


def gram_of(c, mine, theirs):
    halves = in_order(c, mine, theirs)
    return jnp.concatenate([p for h in halves for p in (h[:, :RANK], h[:, RANK:])], axis=0)


def put_message(c, left_ref, piece, out_ref):
    own = left_ref[pl.ds(pl.multiple_of(c * PART, PART), PART)]
    wt = dot(own, piece, 1, 0)
    gram = dot(own, left_ref[...], 1, 1)
    gram = jnp.concatenate([gram[:GRAM], gram[GRAM:]], axis=1)
    for i in range(XY):
        out_ref[i, :PART] = wt
        out_ref[i, PART:] = gram


def half_field(there, base_in, local_in, error_in, base, local, error, sem, out_ref):
    part = HALF // 2
    loads = []
    for i in range(2):
        here = pl.ds(i * part, part)
        rows = pl.ds(pl.multiple_of(there + i * part, part), part)
        for j, (src, dst) in enumerate([(base_in, base), (local_in.at[0], local), (error_in.at[0], error)]):
            load = pltpu.make_async_copy(src.at[rows], dst.at[here], sem.at[i, j])
            load.start()
            loads.append(load)
    for i in range(2):
        here = pl.ds(i * part, part)
        for load in loads[3 * i : 3 * i + 3]:
            load.wait()
        out_ref[here] = base[here] - local[here].astype(F32) + error[here]


def other_half(at_ref, base_in, local_in, error_in, out_ref, base, local, error, sem):
    half_field((1 - at_ref[0]) * HALF, base_in, local_in, error_in, base, local, error, sem, out_ref)


def own_half(at_ref, base_in, local_in, error_in, out_ref, base, local, error, sem):
    half_field(at_ref[0] * HALF, base_in, local_in, error_in, base, local, error, sem, out_ref)


def first_send(mine_ref, theirs_ref, query_ref, out_ref):
    pair = mine_ref[...] + theirs_ref[...]
    left = dot(pair, query_ref[...], 1, 1)
    packed = jnp.concatenate([left[: HALF // 2], left[HALF // 2 :]], axis=1)
    for z in range(NZ):
        out_ref[z, :HALF] = pair[:, z * SLICE : (z + 1) * SLICE]
        out_ref[z, HALF:] = packed


def mean_over_z(got_ref, out_ref):
    out_ref[...] = add_up(got_ref) * (1.0 / REPLICAS)


def first_message(at_ref, mine_ref, theirs_ref, out_ref, piece_ref, left_ref):
    c = at_ref[0]
    halves = in_order(c, mine_ref[...], theirs_ref[...])
    piece = jnp.concatenate([h[:HALF] for h in halves], axis=0)
    left = jnp.concatenate([p for h in halves for p in (h[HALF:, :RANK], h[HALF:, RANK:])], axis=0)
    piece_ref[...] = piece
    left_ref[...] = left.T
    put_message(c, left_ref, piece, out_ref)


def left_parts(got_ref, piece_ref, out_ref, gram_ref):
    total = add_up(got_ref)
    gram_ref[...] = total[PART:]
    left = dot(piece_ref[...], total[:PART], 1, 1)
    packed = jnp.concatenate([left[i * LEFT : (i + 1) * LEFT] for i in range(128 // PART)], axis=1)
    for z in range(NZ):
        out_ref[z] = packed


def factor(at_ref, mine_ref, theirs_ref, out_ref):
    out_ref[...] = inverse_factor(gram_of(at_ref[0], mine_ref[...], theirs_ref[...]))


def total_of(got_ref, inv_ref, out_ref):
    out_ref[...] = add_up(got_ref)


def next_message(at_ref, mine_ref, theirs_ref, inv_ref, piece_ref, out_ref, left_ref):
    c = at_ref[0]
    first, second = in_order(c, mine_ref[...], theirs_ref[...])
    left = jnp.concatenate(
        [
            jnp.concatenate([h[:, i * PART : (i + 1) * PART] for h in (first, second)], axis=1)
            for i in range(128 // PART)
        ],
        axis=0,
    )
    left_ref[...] = dot(inv_ref[...], left, 1, 1)
    put_message(c, left_ref, piece_ref[...], out_ref)


def right_parts(got_ref, out_ref, gram_ref):
    total = add_up(got_ref)
    gram_ref[...] = total[PART:]
    for i in range(ZC):
        out_ref[i] = total[:PART]


def coefficients(at_ref, mine_ref, theirs_ref, left_ref, base_in, mom_in, coef_ref, base_ref, base, mom, sem):
    loads = [
        pltpu.make_async_copy(src, dst, sem.at[i])
        for i, (src, dst) in enumerate([(base_in, base), (mom_in, mom)])
    ]
    for load in loads:
        load.start()
    inv = inverse_factor(gram_of(at_ref[0], mine_ref[...], theirs_ref[...]))
    basis = dot(inv, left_ref[...], 1, 0)
    coef_ref[...] = dot(basis, inv, 0, 0)
    for load in loads:
        load.wait()
    base_ref[...] = base[...] - (outer_rate * momentum_decay * momentum_decay) * mom[...]


def finish(at_ref, full_ref, coef_ref, own, other, base, mom_in, base_out, err_out, mom_out,
           mom, nbase, nerr, nmom, in_sem, out_sem):
    c = at_ref[0]
    part = HALF // 2
    count = ROWS // part
    at = [i * part if i < count // 2 else (i - count // 2) * part for i in range(count)]
    here = [pl.ds(i * part, part) for i in range(count)]
    rows = [
        pl.ds(pl.multiple_of((c if i < count // 2 else 1 - c) * HALF + at[i], part), part)
        for i in range(count)
    ]
    loads = [
        pltpu.make_async_copy(mom_in.at[rows[i]], mom.at[here[i]], in_sem.at[i]) for i in range(count)
    ]
    for load in loads:
        load.start()
    wt = jnp.concatenate(
        [jnp.concatenate([full_ref[z * NC + k] for k in range(NC)], axis=0) for z in range(NZ)], axis=1
    )
    stores = []

    def store(j, i, src, dst):
        copy = pltpu.make_async_copy(src.at[here[i]], dst.at[rows[i]], out_sem.at[j, i])
        copy.start()
        stores.append(copy)

    for i in range(count):
        field = own if i < count // 2 else other
        approx = dot(coef_ref[rows[i]], wt, 1, 0)
        nerr[here[i]] = field[pl.ds(at[i], part)] - approx
        store(0, i, nerr, err_out)
        nbase[here[i]] = base[rows[i]] - (outer_rate * (1.0 + momentum_decay)) * approx
        store(1, i, nbase, base_out)
        loads[i].wait()
        nmom[here[i]] = momentum_decay * mom[here[i]] + approx
        store(2, i, nmom, mom_out)
    for copy in stores:
        copy.wait()


def exchange(operand, axes):
    return lax.all_to_all(operand, axes, 0, 0, tiled=True)


def in_hbm(x):
    return pltpu.with_memory_space_constraint(x, pltpu.HBM)


def in_vmem(x):
    return pltpu.with_memory_space_constraint(x, pltpu.VMEM)


def swap(x):
    return lax.ppermute(x, "c", SWAP)


def body(base, local, error, momentum, query):
    c = lax.axis_index("c")
    at = c.astype(jnp.int32)[None]
    buffers = [pltpu.VMEM((HALF, KV), t) for t in (F32, jnp.bfloat16, F32)]
    buffers.append(pltpu.SemaphoreType.DMA((2, 3)))
    half = lambda kernel: call(kernel, shape(HALF, KV), [SMEM] + [HBM] * 3, buffers)(
        at, in_hbm(base), in_hbm(local), in_hbm(error)
    )
    other = half(other_half)
    theirs = swap(other)
    own = half(own_half)
    send = call(first_send, shape(NZ, HALF + HALF // 2, 128), [VMEM] * 3)(own, theirs, query.T)
    mean = call(mean_over_z, shape(HALF + HALF // 2, 128), [VMEM])(exchange(send, "z"))
    send, piece, left = call(
        first_message, [shape(XY, PACK, 128), shape(ROWS, SLICE), shape(RANK, ROWS)], [SMEM] + [VMEM] * 2
    )(at, mean, swap(mean))
    for step in range(1, ITERS):
        send, gram = call(left_parts, [shape(NZ, LEFT, 128), shape(GRAM, 128)], [VMEM] * 2)(
            exchange(send, ("x", "y")), piece
        )
        got = exchange(send, "z")
        inv = call(factor, shape(RANK, RANK), [SMEM] + [VMEM] * 2, flops=10**9)(at, gram, swap(gram))
        part = call(total_of, shape(LEFT, 128), [VMEM, HBM])(got, inv)
        send, left = call(
            next_message, [shape(XY, PACK, 128), shape(RANK, ROWS)], [SMEM] + [VMEM] * 4
        )(at, part, swap(part), inv, piece)
    send, gram = call(right_parts, [shape(ZC, PART, 128), shape(GRAM, 128)], [VMEM])(
        exchange(send, ("x", "y"))
    )
    full = exchange(send, ("z", "c"))
    whole = shape(ROWS, KV)
    big = pltpu.VMEM((ROWS, KV), F32)
    coef, partial_base = call(
        coefficients,
        [shape(ROWS, RANK), whole],
        [SMEM] + [VMEM] * 3 + [HBM] * 2,
        [big] * 2 + [pltpu.SemaphoreType.DMA((2,))],
        flops=10**9,
    )(at, gram, swap(gram), left, in_hbm(base), in_hbm(momentum))
    new_base, new_error, new_momentum = pl.pallas_call(
        finish,
        out_shape=[whole] * 3,
        in_specs=[SMEM] + [VMEM] * 5 + [HBM],
        out_specs=[HBM] * 3,
        scratch_shapes=[big] * 4 + [pltpu.SemaphoreType.DMA((4,)), pltpu.SemaphoreType.DMA((3, 4))],
        compiler_params=pltpu.CompilerParams(vmem_limit_bytes=16 * 2**20),
    )(at, full, coef, in_vmem(own), in_vmem(other), in_vmem(partial_base), in_hbm(momentum))
    return new_base, new_error[None], new_momentum


def solution(mesh):
    mesh = Mesh(mesh.devices.reshape(NZ, NC, NX, NY), ("z", "c", "x", "y"))
    outer, shard = ("z", "c"), ("x", "y")
    in_specs = (
        P(shard, None),
        P(outer, shard, None),
        P(outer, shard, None),
        P(shard, None),
        P(),
    )
    out_specs = (P(shard, None), P(outer, shard, None), P(shard, None))
    return jax.shard_map(body, mesh=mesh, in_specs=in_specs, out_specs=out_specs, check_vma=False)
```

```python
import functools
import jax
import jax.numpy as jnp
from jax import lax
from jax.experimental import pallas as pl
from jax.experimental.pallas import tpu as pltpu
from jax.sharding import Mesh, PartitionSpec as P

ITERS = 2
REPLICAS = 16
RANK = 64
NZ, NC, NX, NY = 8, 2, 4, 4
NH = NZ // 2
Z = ("h", "l")
XY, ZC = NX * NY, NZ * NC
ROWS = 320
HALF = ROWS // 2
KV = 1024
SLICE = KV // NZ
PART = RANK // NC
LEFT = ROWS * PART // 128
GRAM = PART * RANK // 128
PACK = PART + GRAM

momentum_decay = 0.9
outer_rate = 0.7

HI = lax.Precision.HIGHEST
SWAP = [(0, 1), (1, 0)]
PAIRS = (
    [(i, i ^ 1) for i in range(NZ)],
    [(i, (i + 1 if i % 2 else i - 1) % NZ) for i in range(NZ)],
)
PAIRED = HALF // 2
F32 = jnp.float32
VMEM = pl.BlockSpec(memory_space=pltpu.VMEM)
SMEM = pl.BlockSpec(memory_space=pltpu.SMEM)
HBM = pl.BlockSpec(memory_space=pltpu.HBM)


def shape(*dims):
    return jax.ShapeDtypeStruct(dims, F32)


def call(kernel, outs, ins, scratch=(), mib=8, flops=10**6):
    return pl.pallas_call(
        kernel,
        out_shape=outs,
        in_specs=ins,
        out_specs=jax.tree.map(lambda _: VMEM, outs),
        scratch_shapes=list(scratch),
        compiler_params=pltpu.CompilerParams(vmem_limit_bytes=mib * 2**20),
        cost_estimate=pl.CostEstimate(flops=flops, bytes_accessed=2**20, transcendentals=0),
    )


def dot(a, b, ca, cb):
    return lax.dot_general(a, b, (((ca,), (cb,)), ((), ())), precision=HI, preferred_element_type=F32)


def add_up(ref):
    return functools.reduce(lambda a, b: a + b, [ref[i] for i in range(ref.shape[0])])


def spread(x):
    return jnp.broadcast_to(x, (8, 128))


def inverse_factor(gram):
    n = RANK // 8
    eye = (
        lax.broadcasted_iota(jnp.int32, (RANK, RANK), 0)
        == lax.broadcasted_iota(jnp.int32, (RANK, RANK), 1)
    ).astype(F32)
    full = jnp.concatenate([gram, eye], axis=1)
    a = [full[8 * i : 8 * i + 8] for i in range(n)]
    sub = lax.broadcasted_iota(jnp.int32, (8, 128), 0)
    for b in range(n):
        p = a[b]
        at = 8 * b
        e = [spread(p[:, at + j : at + j + 1]) for j in range(8)]
        cols = [[spread(a[i][:, at + j : at + j + 1]) for j in range(8)] for i in range(b + 1, n)]
        for k in range(8):
            s = lax.rsqrt(spread(e[k][k : k + 1]))
            f = jnp.where(sub > k, e[k] * (s * s), 0.0)
            u = [None] * 8
            for j in range(k + 1, 8):
                row = spread(e[j][k : k + 1])
                u[j] = row * s
                e[j] = e[j] - f * row
            prow = spread(p[k : k + 1])
            p = jnp.where(sub == k, prow * s, p - f * prow)
            for ci in cols:
                ci[k] = ci[k] * s
                for j in range(k + 1, 8):
                    ci[j] = ci[j] - ci[k] * u[j]
        for i in range(b + 1, n):
            for k in range(8):
                a[i] = a[i] - cols[i - b - 1][k] * spread(p[k : k + 1])
        a[b] = p
    return jnp.concatenate(a, axis=0)[:, RANK:]


def in_order(c, mine, theirs):
    first = c == 0
    return jnp.where(first, mine, theirs), jnp.where(first, theirs, mine)


def gram_of(c, mine, theirs):
    halves = in_order(c, mine, theirs)
    return jnp.concatenate([p for h in halves for p in (h[:, :RANK], h[:, RANK:])], axis=0)


def put_message(c, left_ref, piece, out_ref):
    own = left_ref[pl.ds(pl.multiple_of(c * PART, PART), PART)]
    wt = dot(own, piece, 1, 0)
    gram = dot(own, left_ref[...], 1, 1)
    gram = jnp.concatenate([gram[:GRAM], gram[GRAM:]], axis=1)
    for i in range(XY):
        out_ref[i, :PART] = wt
        out_ref[i, PART:] = gram


def half_field(there, base_in, local_in, error_in, base, local, error, sem, out_ref):
    part = HALF // 2
    loads = []
    for i in range(2):
        here = pl.ds(i * part, part)
        rows = pl.ds(pl.multiple_of(there + i * part, part), part)
        for j, (src, dst) in enumerate([(base_in, base), (local_in.at[0], local), (error_in.at[0], error)]):
            load = pltpu.make_async_copy(src.at[rows], dst.at[here], sem.at[i, j])
            load.start()
            loads.append(load)
    for i in range(2):
        here = pl.ds(i * part, part)
        for load in loads[3 * i : 3 * i + 3]:
            load.wait()
        out_ref[here] = base[here] - local[here].astype(F32) + error[here]


def other_half(at_ref, base_in, local_in, error_in, out_ref, base, local, error, sem):
    half_field((1 - at_ref[0]) * HALF, base_in, local_in, error_in, base, local, error, sem, out_ref)


def own_half(at_ref, base_in, local_in, error_in, out_ref, base, local, error, sem):
    half_field(at_ref[0] * HALF, base_in, local_in, error_in, base, local, error, sem, out_ref)


def first_send(low_ref, mine_ref, theirs_ref, query_ref, keep_ref, left_ref, first_ref, second_ref, pair_ref):
    pair_ref[...] = mine_ref[...] + theirs_ref[...]
    low = low_ref[0]
    for h in range(NH):
        slices = [pl.ds(pl.multiple_of((2 * h + l) * SLICE, SLICE), SLICE) for l in (low, 1 - low)]
        keep_ref[h] = pair_ref[:, slices[0]]
        for i, ref in enumerate((first_ref, second_ref)):
            ref[pl.ds(h * PAIRED, PAIRED)] = pair_ref[pl.ds(i * PAIRED, PAIRED), slices[1]]
    left = dot(pair_ref[...], query_ref[...], 1, 1)
    n = PAIRED // 2
    for i, ref in enumerate((first_ref, second_ref)):
        at = i * PAIRED
        packed = jnp.concatenate([left[at : at + n], left[at + n : at + 2 * n]], axis=1)
        ref[NH * PAIRED :] = packed
        left_ref[i * n : (i + 1) * n] = packed


def fold(keep_ref, left_ref, first_ref, second_ref, out_ref):
    n = PAIRED // 2
    for i, ref in enumerate((first_ref, second_ref)):
        rows = slice(i * PAIRED, (i + 1) * PAIRED)
        for h in range(NH):
            out_ref[h, rows] = keep_ref[h, rows] + ref[h * PAIRED : (h + 1) * PAIRED]
        packed = left_ref[i * n : (i + 1) * n] + ref[NH * PAIRED :]
        for h in range(NH):
            out_ref[h, HALF + i * n : HALF + (i + 1) * n] = packed


def mean_over_z(got_ref, out_ref):
    out_ref[...] = add_up(got_ref) * (1.0 / REPLICAS)


def first_message(at_ref, mine_ref, theirs_ref, out_ref, piece_ref, left_ref):
    c = at_ref[0]
    halves = in_order(c, mine_ref[...], theirs_ref[...])
    piece = jnp.concatenate([h[:HALF] for h in halves], axis=0)
    n = PAIRED // 2
    left = jnp.concatenate(
        [
            h[at : at + n, lanes]
            for h in halves
            for at in (HALF, HALF + n)
            for lanes in (slice(0, RANK), slice(RANK, 2 * RANK))
        ],
        axis=0,
    )
    piece_ref[...] = piece
    left_ref[...] = left.T
    put_message(c, left_ref, piece, out_ref)


def left_parts(got_ref, piece_ref, out_ref, gram_ref):
    total = add_up(got_ref)
    gram_ref[...] = total[PART:]
    left = dot(piece_ref[...], total[:PART], 1, 1)
    packed = jnp.concatenate([left[i * LEFT : (i + 1) * LEFT] for i in range(128 // PART)], axis=1)
    for z in range(NZ):
        out_ref[z] = packed


def factor(at_ref, mine_ref, theirs_ref, out_ref):
    out_ref[...] = inverse_factor(gram_of(at_ref[0], mine_ref[...], theirs_ref[...]))


def total_of(got_ref, inv_ref, out_ref):
    out_ref[...] = add_up(got_ref)


def next_message(at_ref, mine_ref, theirs_ref, inv_ref, piece_ref, out_ref, left_ref):
    c = at_ref[0]
    first, second = in_order(c, mine_ref[...], theirs_ref[...])
    left = jnp.concatenate(
        [
            jnp.concatenate([h[:, i * PART : (i + 1) * PART] for h in (first, second)], axis=1)
            for i in range(128 // PART)
        ],
        axis=0,
    )
    left_ref[...] = dot(inv_ref[...], left, 1, 1)
    put_message(c, left_ref, piece_ref[...], out_ref)


def right_parts(got_ref, out_ref, gram_ref):
    total = add_up(got_ref)
    gram_ref[...] = total[PART:]
    for i in range(ZC):
        out_ref[i] = total[:PART]


def coefficients(at_ref, mine_ref, theirs_ref, left_ref, base_in, mom_in, coef_ref, base_ref, base, mom, sem):
    loads = [
        pltpu.make_async_copy(src, dst, sem.at[i])
        for i, (src, dst) in enumerate([(base_in, base), (mom_in, mom)])
    ]
    for load in loads:
        load.start()
    inv = inverse_factor(gram_of(at_ref[0], mine_ref[...], theirs_ref[...]))
    basis = dot(inv, left_ref[...], 1, 0)
    coef_ref[...] = dot(basis, inv, 0, 0)
    for load in loads:
        load.wait()
    base_ref[...] = base[...] - (outer_rate * momentum_decay * momentum_decay) * mom[...]


def finish(at_ref, full_ref, coef_ref, own, other, base, mom_in, base_out, err_out, mom_out,
           mom, nbase, nerr, nmom, in_sem, out_sem):
    c = at_ref[0]
    part = HALF // 2
    count = ROWS // part
    at = [i * part if i < count // 2 else (i - count // 2) * part for i in range(count)]
    here = [pl.ds(i * part, part) for i in range(count)]
    rows = [
        pl.ds(pl.multiple_of((c if i < count // 2 else 1 - c) * HALF + at[i], part), part)
        for i in range(count)
    ]
    loads = [
        pltpu.make_async_copy(mom_in.at[rows[i]], mom.at[here[i]], in_sem.at[i]) for i in range(count)
    ]
    for load in loads:
        load.start()
    wt = jnp.concatenate(
        [jnp.concatenate([full_ref[z * NC + k] for k in range(NC)], axis=0) for z in range(NZ)], axis=1
    )
    stores = []

    def store(j, i, src, dst):
        copy = pltpu.make_async_copy(src.at[here[i]], dst.at[rows[i]], out_sem.at[j, i])
        copy.start()
        stores.append(copy)

    for i in range(count):
        field = own if i < count // 2 else other
        approx = dot(coef_ref[rows[i]], wt, 1, 0)
        nerr[here[i]] = field[pl.ds(at[i], part)] - approx
        store(0, i, nerr, err_out)
        nbase[here[i]] = base[rows[i]] - (outer_rate * (1.0 + momentum_decay)) * approx
        store(1, i, nbase, base_out)
        loads[i].wait()
        nmom[here[i]] = momentum_decay * mom[here[i]] + approx
        store(2, i, nmom, mom_out)
    for copy in stores:
        copy.wait()


def exchange(operand, axes):
    return lax.all_to_all(operand, axes, 0, 0, tiled=True)


def in_hbm(x):
    return pltpu.with_memory_space_constraint(x, pltpu.HBM)


def in_vmem(x):
    return pltpu.with_memory_space_constraint(x, pltpu.VMEM)


def swap(x):
    return lax.ppermute(x, "c", SWAP)


def body(base, local, error, momentum, query):
    c = lax.axis_index("c")
    at = c.astype(jnp.int32)[None]
    low = lax.axis_index("l").astype(jnp.int32)[None]
    buffers = [pltpu.VMEM((HALF, KV), t) for t in (F32, jnp.bfloat16, F32)]
    buffers.append(pltpu.SemaphoreType.DMA((2, 3)))
    half = lambda kernel: call(kernel, shape(HALF, KV), [SMEM] + [HBM] * 3, buffers)(
        at, in_hbm(base), in_hbm(local), in_hbm(error)
    )
    other = half(other_half)
    theirs = swap(other)
    own = half(own_half)
    message = shape(NH * PAIRED + PAIRED // 2, 128)
    keep, left, first, second = call(
        first_send,
        [shape(NH, HALF, SLICE), shape(HALF // 2, 128), message, message],
        [SMEM] + [VMEM] * 3,
        [pltpu.VMEM((HALF, KV), F32)],
    )(low, own, theirs, query.T)
    first = lax.ppermute(first, Z, PAIRS[0])
    second = lax.ppermute(second, Z, PAIRS[1])
    send = call(fold, shape(NH, HALF + HALF // 2, 128), [VMEM] * 4)(keep, left, first, second)
    mean = call(mean_over_z, shape(HALF + HALF // 2, 128), [VMEM])(exchange(send, "h"))
    send, piece, left = call(
        first_message, [shape(XY, PACK, 128), shape(ROWS, SLICE), shape(RANK, ROWS)], [SMEM] + [VMEM] * 2
    )(at, mean, swap(mean))
    for step in range(1, ITERS):
        send, gram = call(left_parts, [shape(NZ, LEFT, 128), shape(GRAM, 128)], [VMEM] * 2)(
            exchange(send, ("x", "y")), piece
        )
        got = exchange(send, Z)
        inv = call(factor, shape(RANK, RANK), [SMEM] + [VMEM] * 2, flops=10**9)(at, gram, swap(gram))
        part = call(total_of, shape(LEFT, 128), [VMEM, HBM])(got, inv)
        send, left = call(
            next_message, [shape(XY, PACK, 128), shape(RANK, ROWS)], [SMEM] + [VMEM] * 4
        )(at, part, swap(part), inv, piece)
    send, gram = call(right_parts, [shape(ZC, PART, 128), shape(GRAM, 128)], [VMEM])(
        exchange(send, ("x", "y"))
    )
    full = exchange(send, Z + ("c",))
    whole = shape(ROWS, KV)
    big = pltpu.VMEM((ROWS, KV), F32)
    coef, partial_base = call(
        coefficients,
        [shape(ROWS, RANK), whole],
        [SMEM] + [VMEM] * 3 + [HBM] * 2,
        [big] * 2 + [pltpu.SemaphoreType.DMA((2,))],
        flops=10**9,
    )(at, gram, swap(gram), left, in_hbm(base), in_hbm(momentum))
    new_base, new_error, new_momentum = pl.pallas_call(
        finish,
        out_shape=[whole] * 3,
        in_specs=[SMEM] + [VMEM] * 5 + [HBM],
        out_specs=[HBM] * 3,
        scratch_shapes=[big] * 4 + [pltpu.SemaphoreType.DMA((4,)), pltpu.SemaphoreType.DMA((3, 4))],
        compiler_params=pltpu.CompilerParams(vmem_limit_bytes=16 * 2**20),
    )(at, full, coef, in_vmem(own), in_vmem(other), in_vmem(partial_base), in_hbm(momentum))
    return new_base, new_error[None], new_momentum


def solution(mesh):
    mesh = Mesh(mesh.devices.reshape(NH, 2, NC, NX, NY), ("h", "l", "c", "x", "y"))
    outer, shard = ("h", "l", "c"), ("x", "y")
    in_specs = (
        P(shard, None),
        P(outer, shard, None),
        P(outer, shard, None),
        P(shard, None),
        P(),
    )
    out_specs = (P(shard, None), P(outer, shard, None), P(shard, None))
    return jax.shard_map(body, mesh=mesh, in_specs=in_specs, out_specs=out_specs, check_vma=False)
```

```python
import functools
import jax
import jax.numpy as jnp
from jax import lax
from jax.experimental import pallas as pl
from jax.experimental.pallas import tpu as pltpu
from jax.sharding import Mesh, PartitionSpec as P

ITERS = 2
REPLICAS = 16
RANK = 64
NZ, NC, NX, NY = 8, 2, 4, 4
NH = NZ // 2
Z = ("h", "l")
XY, ZC = NX * NY, NZ * NC
ROWS = 320
HALF = ROWS // 2
KV = 1024
SLICE = KV // NZ
PART = RANK // NC
LEFT = ROWS * PART // 128
GRAM = PART * RANK // 128
PACK = PART + GRAM

momentum_decay = 0.9
outer_rate = 0.7

HI = lax.Precision.HIGHEST
SWAP = [(0, 1), (1, 0)]
PAIRS = (
    [(i, i ^ 1) for i in range(NZ)],
    [(i, (i + 1 if i % 2 else i - 1) % NZ) for i in range(NZ)],
)
PAIRED = HALF // 2
F32 = jnp.float32
VMEM = pl.BlockSpec(memory_space=pltpu.VMEM)
SMEM = pl.BlockSpec(memory_space=pltpu.SMEM)
HBM = pl.BlockSpec(memory_space=pltpu.HBM)


def shape(*dims):
    return jax.ShapeDtypeStruct(dims, F32)


def call(kernel, outs, ins, scratch=(), mib=8, flops=10**6):
    return pl.pallas_call(
        kernel,
        out_shape=outs,
        in_specs=ins,
        out_specs=jax.tree.map(lambda _: VMEM, outs),
        scratch_shapes=list(scratch),
        compiler_params=pltpu.CompilerParams(vmem_limit_bytes=mib * 2**20),
        cost_estimate=pl.CostEstimate(flops=flops, bytes_accessed=2**20, transcendentals=0),
    )


def dot(a, b, ca, cb):
    return lax.dot_general(a, b, (((ca,), (cb,)), ((), ())), precision=HI, preferred_element_type=F32)


def add_up(ref):
    return functools.reduce(lambda a, b: a + b, [ref[i] for i in range(ref.shape[0])])


def spread(x):
    return jnp.broadcast_to(x, (8, 128))


def inverse_factor(gram):
    n = RANK // 8
    eye = (
        lax.broadcasted_iota(jnp.int32, (RANK, RANK), 0)
        == lax.broadcasted_iota(jnp.int32, (RANK, RANK), 1)
    ).astype(F32)
    full = jnp.concatenate([gram, eye], axis=1)
    a = [full[8 * i : 8 * i + 8] for i in range(n)]
    sub = lax.broadcasted_iota(jnp.int32, (8, 128), 0)
    for b in range(n):
        p = a[b]
        at = 8 * b
        e = [spread(p[:, at + j : at + j + 1]) for j in range(8)]
        cols = [[spread(a[i][:, at + j : at + j + 1]) for j in range(8)] for i in range(b + 1, n)]
        for k in range(8):
            s = lax.rsqrt(spread(e[k][k : k + 1]))
            f = jnp.where(sub > k, e[k] * (s * s), 0.0)
            u = [None] * 8
            for j in range(k + 1, 8):
                row = spread(e[j][k : k + 1])
                u[j] = row * s
                e[j] = e[j] - f * row
            prow = spread(p[k : k + 1])
            p = jnp.where(sub == k, prow * s, p - f * prow)
            for ci in cols:
                ci[k] = ci[k] * s
                for j in range(k + 1, 8):
                    ci[j] = ci[j] - ci[k] * u[j]
        for i in range(b + 1, n):
            for k in range(8):
                a[i] = a[i] - cols[i - b - 1][k] * spread(p[k : k + 1])
        a[b] = p
    return jnp.concatenate(a, axis=0)[:, RANK:]


def in_order(c, mine, theirs):
    first = c == 0
    return jnp.where(first, mine, theirs), jnp.where(first, theirs, mine)


def gram_of(c, mine, theirs):
    halves = in_order(c, mine, theirs)
    return jnp.concatenate([p for h in halves for p in (h[:, :RANK], h[:, RANK:])], axis=0)


def put_message(c, left_ref, piece, out_ref):
    own = left_ref[pl.ds(pl.multiple_of(c * PART, PART), PART)]
    wt = dot(own, piece, 1, 0)
    gram = dot(own, left_ref[...], 1, 1)
    gram = jnp.concatenate([gram[:GRAM], gram[GRAM:]], axis=1)
    for i in range(XY):
        out_ref[i, :PART] = wt
        out_ref[i, PART:] = gram


def half_field(there, base_in, local_in, error_in, base, local, error, sem, out_ref):
    part = HALF // 2
    loads = []
    for i in range(2):
        here = pl.ds(i * part, part)
        rows = pl.ds(pl.multiple_of(there + i * part, part), part)
        for j, (src, dst) in enumerate([(base_in, base), (local_in.at[0], local), (error_in.at[0], error)]):
            load = pltpu.make_async_copy(src.at[rows], dst.at[here], sem.at[i, j])
            load.start()
            loads.append(load)
    for i in range(2):
        here = pl.ds(i * part, part)
        for load in loads[3 * i : 3 * i + 3]:
            load.wait()
        out_ref[here] = base[here] - local[here].astype(F32) + error[here]


def other_half(at_ref, base_in, local_in, error_in, out_ref, base, local, error, sem):
    half_field((1 - at_ref[0]) * HALF, base_in, local_in, error_in, base, local, error, sem, out_ref)


def own_half(at_ref, base_in, local_in, error_in, out_ref, base, local, error, sem):
    half_field(at_ref[0] * HALF, base_in, local_in, error_in, base, local, error, sem, out_ref)


def first_send(low_ref, mine_ref, theirs_ref, query_ref, keep_ref, left_ref, first_ref, second_ref, pair_ref):
    pair_ref[...] = mine_ref[...] + theirs_ref[...]
    low = low_ref[0]
    for h in range(NH):
        slices = [pl.ds(pl.multiple_of((2 * h + l) * SLICE, SLICE), SLICE) for l in (low, 1 - low)]
        keep_ref[h] = pair_ref[:, slices[0]]
        for i, ref in enumerate((first_ref, second_ref)):
            ref[pl.ds(h * PAIRED, PAIRED)] = pair_ref[pl.ds(i * PAIRED, PAIRED), slices[1]]
    left = dot(pair_ref[...], query_ref[...], 1, 1)
    n = PAIRED // 2
    for i, ref in enumerate((first_ref, second_ref)):
        at = i * PAIRED
        packed = jnp.concatenate([left[at : at + n], left[at + n : at + 2 * n]], axis=1)
        ref[NH * PAIRED :] = packed
        left_ref[i * n : (i + 1) * n] = packed


def fold(high_ref, keep_ref, left_ref, first_ref, second_ref, mine_ref, *out_refs):
    out_ref = out_refs[-1]
    out_refs = (mine_ref,) + out_refs[:-1]
    n = PAIRED // 2
    for i, ref in enumerate((first_ref, second_ref)):
        rows = slice(i * PAIRED, (i + 1) * PAIRED)
        for h in range(NH):
            out_ref[h, rows] = keep_ref[h, rows] + ref[h * PAIRED : (h + 1) * PAIRED]
        packed = left_ref[i * n : (i + 1) * n] + ref[NH * PAIRED :]
        for ref in out_refs:
            ref[HALF + i * n : HALF + (i + 1) * n] = packed
    for k, ref in enumerate(out_refs):
        ref[:HALF] = out_ref[lax.rem(high_ref[0] + k, NH)]


def sum_of_four(refs):
    own, across, one, three = [ref[...] for ref in refs]
    return (own + across) + (one + three)


def mean_over_z(*refs):
    refs[-1][...] = sum_of_four(refs[:-1]) * (1.0 / REPLICAS)


def total_of_four(*refs):
    refs[-1][...] = sum_of_four(refs[:-1])


def first_message(at_ref, mine_ref, theirs_ref, out_ref, piece_ref, left_ref):
    c = at_ref[0]
    halves = in_order(c, mine_ref[...], theirs_ref[...])
    piece = jnp.concatenate([h[:HALF] for h in halves], axis=0)
    n = PAIRED // 2
    left = jnp.concatenate(
        [
            h[at : at + n, lanes]
            for h in halves
            for at in (HALF, HALF + n)
            for lanes in (slice(0, RANK), slice(RANK, 2 * RANK))
        ],
        axis=0,
    )
    piece_ref[...] = piece
    left_ref[...] = left.T
    put_message(c, left_ref, piece, out_ref)


def left_parts(got_ref, piece_ref, out_ref, gram_ref):
    total = add_up(got_ref)
    gram_ref[...] = total[PART:]
    left = dot(piece_ref[...], total[:PART], 1, 1)
    packed = jnp.concatenate([left[i * LEFT : (i + 1) * LEFT] for i in range(128 // PART)], axis=1)
    for z in range(NZ):
        out_ref[z] = packed


def factor(at_ref, mine_ref, theirs_ref, out_ref):
    out_ref[...] = inverse_factor(gram_of(at_ref[0], mine_ref[...], theirs_ref[...]))


def total_of(got_ref, inv_ref, out_ref):
    out_ref[...] = add_up(got_ref)


def next_message(at_ref, mine_ref, theirs_ref, inv_ref, piece_ref, out_ref, left_ref):
    c = at_ref[0]
    first, second = in_order(c, mine_ref[...], theirs_ref[...])
    left = jnp.concatenate(
        [
            jnp.concatenate([h[:, i * PART : (i + 1) * PART] for h in (first, second)], axis=1)
            for i in range(128 // PART)
        ],
        axis=0,
    )
    left_ref[...] = dot(inv_ref[...], left, 1, 1)
    put_message(c, left_ref, piece_ref[...], out_ref)


def right_parts(got_ref, out_ref, gram_ref):
    total = add_up(got_ref)
    gram_ref[...] = total[PART:]
    for i in range(ZC):
        out_ref[i] = total[:PART]


def coefficients(at_ref, mine_ref, theirs_ref, left_ref, base_in, mom_in, coef_ref, base_ref, base, mom, sem):
    loads = [
        pltpu.make_async_copy(src, dst, sem.at[i])
        for i, (src, dst) in enumerate([(base_in, base), (mom_in, mom)])
    ]
    for load in loads:
        load.start()
    inv = inverse_factor(gram_of(at_ref[0], mine_ref[...], theirs_ref[...]))
    basis = dot(inv, left_ref[...], 1, 0)
    coef_ref[...] = dot(basis, inv, 0, 0)
    for load in loads:
        load.wait()
    base_ref[...] = base[...] - (outer_rate * momentum_decay * momentum_decay) * mom[...]


def finish(at_ref, full_ref, coef_ref, own, other, base, mom_in, base_out, err_out, mom_out,
           mom, nbase, nerr, nmom, in_sem, out_sem):
    c = at_ref[0]
    part = HALF // 2
    count = ROWS // part
    at = [i * part if i < count // 2 else (i - count // 2) * part for i in range(count)]
    here = [pl.ds(i * part, part) for i in range(count)]
    rows = [
        pl.ds(pl.multiple_of((c if i < count // 2 else 1 - c) * HALF + at[i], part), part)
        for i in range(count)
    ]
    loads = [
        pltpu.make_async_copy(mom_in.at[rows[i]], mom.at[here[i]], in_sem.at[i]) for i in range(count)
    ]
    for load in loads:
        load.start()
    wt = jnp.concatenate(
        [jnp.concatenate([full_ref[z * NC + k] for k in range(NC)], axis=0) for z in range(NZ)], axis=1
    )
    stores = []

    def store(j, i, src, dst):
        copy = pltpu.make_async_copy(src.at[here[i]], dst.at[rows[i]], out_sem.at[j, i])
        copy.start()
        stores.append(copy)

    for i in range(count):
        field = own if i < count // 2 else other
        approx = dot(coef_ref[rows[i]], wt, 1, 0)
        nerr[here[i]] = field[pl.ds(at[i], part)] - approx
        store(0, i, nerr, err_out)
        nbase[here[i]] = base[rows[i]] - (outer_rate * (1.0 + momentum_decay)) * approx
        store(1, i, nbase, base_out)
        loads[i].wait()
        nmom[here[i]] = momentum_decay * mom[here[i]] + approx
        store(2, i, nmom, mom_out)
    for copy in stores:
        copy.wait()


def exchange(operand, axes):
    return lax.all_to_all(operand, axes, 0, 0, tiled=True)


def in_hbm(x):
    return pltpu.with_memory_space_constraint(x, pltpu.HBM)


def in_vmem(x):
    return pltpu.with_memory_space_constraint(x, pltpu.VMEM)


def ring(sends, axis):
    return [lax.ppermute(sends[k - 1], axis, [(i, (i + k) % 4) for i in range(4)]) for k in (2, 1, 3)]


def swap(x):
    return lax.ppermute(x, "c", SWAP)


def body(base, local, error, momentum, query):
    c = lax.axis_index("c")
    at = c.astype(jnp.int32)[None]
    low = lax.axis_index("l").astype(jnp.int32)[None]
    buffers = [pltpu.VMEM((HALF, KV), t) for t in (F32, jnp.bfloat16, F32)]
    buffers.append(pltpu.SemaphoreType.DMA((2, 3)))
    half = lambda kernel: call(kernel, shape(HALF, KV), [SMEM] + [HBM] * 3, buffers)(
        at, in_hbm(base), in_hbm(local), in_hbm(error)
    )
    other = half(other_half)
    theirs = swap(other)
    own = half(own_half)
    message = shape(NH * PAIRED + PAIRED // 2, 128)
    keep, left, first, second = call(
        first_send,
        [shape(NH, HALF, SLICE), shape(HALF // 2, 128), message, message],
        [SMEM] + [VMEM] * 3,
        [pltpu.VMEM((HALF, KV), F32)],
    )(low, own, theirs, query.T)
    first = lax.ppermute(first, Z, PAIRS[0])
    second = lax.ppermute(second, Z, PAIRS[1])
    high = lax.axis_index("h").astype(jnp.int32)[None]
    chunk = shape(HALF + HALF // 2, 128)
    mine, *sends = call(fold, [chunk] * NH, [SMEM] + [VMEM] * 4, [pltpu.VMEM((NH, HALF, SLICE), F32)])(
        high, keep, left, first, second
    )
    mean = call(mean_over_z, chunk, [VMEM] * NH)(mine, *ring(sends, "h"))
    send, piece, left = call(
        first_message, [shape(XY, PACK, 128), shape(ROWS, SLICE), shape(RANK, ROWS)], [SMEM] + [VMEM] * 2
    )(at, mean, swap(mean))
    for step in range(1, ITERS):
        send, gram = call(left_parts, [shape(NZ, LEFT, 128), shape(GRAM, 128)], [VMEM] * 2)(
            exchange(send, ("x", "y")), piece
        )
        got = exchange(send, Z)
        inv = call(factor, shape(RANK, RANK), [SMEM] + [VMEM] * 2, flops=10**9)(at, gram, swap(gram))
        part = call(total_of, shape(LEFT, 128), [VMEM, HBM])(got, inv)
        send, left = call(
            next_message, [shape(XY, PACK, 128), shape(RANK, ROWS)], [SMEM] + [VMEM] * 4
        )(at, part, swap(part), inv, piece)
    send, gram = call(right_parts, [shape(ZC, PART, 128), shape(GRAM, 128)], [VMEM])(
        exchange(send, ("x", "y"))
    )
    full = exchange(in_vmem(send), Z + ("c",))
    whole = shape(ROWS, KV)
    big = pltpu.VMEM((ROWS, KV), F32)
    coef, partial_base = call(
        coefficients,
        [shape(ROWS, RANK), whole],
        [SMEM] + [VMEM] * 3 + [HBM] * 2,
        [big] * 2 + [pltpu.SemaphoreType.DMA((2,))],
        flops=10**9,
    )(at, gram, swap(gram), left, in_hbm(base), in_hbm(momentum))
    new_base, new_error, new_momentum = pl.pallas_call(
        finish,
        out_shape=[whole] * 3,
        in_specs=[SMEM] + [VMEM] * 5 + [HBM],
        out_specs=[HBM] * 3,
        scratch_shapes=[big] * 4 + [pltpu.SemaphoreType.DMA((4,)), pltpu.SemaphoreType.DMA((3, 4))],
        compiler_params=pltpu.CompilerParams(vmem_limit_bytes=16 * 2**20),
    )(at, full, coef, in_vmem(own), in_vmem(other), in_vmem(partial_base), in_hbm(momentum))
    return new_base, new_error[None], new_momentum


def solution(mesh):
    mesh = Mesh(mesh.devices.reshape(NH, 2, NC, NX, NY), ("h", "l", "c", "x", "y"))
    outer, shard = ("h", "l", "c"), ("x", "y")
    in_specs = (
        P(shard, None),
        P(outer, shard, None),
        P(outer, shard, None),
        P(shard, None),
        P(),
    )
    out_specs = (P(shard, None), P(outer, shard, None), P(shard, None))
    return jax.shard_map(body, mesh=mesh, in_specs=in_specs, out_specs=out_specs, check_vma=False)
```

```python
import functools
import jax
import jax.numpy as jnp
from jax import lax
from jax.experimental import pallas as pl
from jax.experimental.pallas import tpu as pltpu
from jax.sharding import Mesh, PartitionSpec as P

ITERS = 2
REPLICAS = 16
RANK = 64
NZ, NC, NX, NY = 8, 2, 4, 4
NH = NZ // 2
Z = ("h", "l")
XY, ZC = NX * NY, NZ * NC
ROWS = 320
HALF = ROWS // 2
KV = 1024
SLICE = KV // NZ
PART = RANK // NC
LEFT = ROWS * PART // 128
GRAM = PART * RANK // 128
PACK = PART + GRAM

momentum_decay = 0.9
outer_rate = 0.7

HI = lax.Precision.HIGHEST
SWAP = [(0, 1), (1, 0)]
PAIRS = (
    [(i, i ^ 1) for i in range(NZ)],
    [(i, (i + 1 if i % 2 else i - 1) % NZ) for i in range(NZ)],
)
PAIRED = HALF // 2
F32 = jnp.float32
VMEM = pl.BlockSpec(memory_space=pltpu.VMEM)
SMEM = pl.BlockSpec(memory_space=pltpu.SMEM)
HBM = pl.BlockSpec(memory_space=pltpu.HBM)


def shape(*dims):
    return jax.ShapeDtypeStruct(dims, F32)


def call(kernel, outs, ins, scratch=(), mib=8, flops=10**6):
    return pl.pallas_call(
        kernel,
        out_shape=outs,
        in_specs=ins,
        out_specs=jax.tree.map(lambda _: VMEM, outs),
        scratch_shapes=list(scratch),
        compiler_params=pltpu.CompilerParams(vmem_limit_bytes=mib * 2**20),
        cost_estimate=pl.CostEstimate(flops=flops, bytes_accessed=2**20, transcendentals=0),
    )


def dot(a, b, ca, cb):
    return lax.dot_general(a, b, (((ca,), (cb,)), ((), ())), precision=HI, preferred_element_type=F32)


def split(x):
    high = x.astype(jnp.bfloat16)
    return high, (x - high.astype(F32)).astype(jnp.bfloat16)


def dot3(a, b, ca, cb):
    (ah, al), (bh, bl) = split(a), split(b)
    one = lambda x, y: lax.dot_general(x, y, (((ca,), (cb,)), ((), ())), preferred_element_type=F32)
    return one(ah, bh) + (one(al, bh) + one(ah, bl))


def add_up(ref):
    return functools.reduce(lambda a, b: a + b, [ref[i] for i in range(ref.shape[0])])


def spread(x):
    return jnp.broadcast_to(x, (8, 128))


def inverse_factor(gram):
    n = RANK // 8
    eye = (
        lax.broadcasted_iota(jnp.int32, (RANK, RANK), 0)
        == lax.broadcasted_iota(jnp.int32, (RANK, RANK), 1)
    ).astype(F32)
    full = jnp.concatenate([gram, eye], axis=1)
    a = [full[8 * i : 8 * i + 8] for i in range(n)]
    sub = lax.broadcasted_iota(jnp.int32, (8, 128), 0)
    for b in range(n):
        p = a[b]
        at = 8 * b
        e = [spread(p[:, at + j : at + j + 1]) for j in range(8)]
        cols = [[spread(a[i][:, at + j : at + j + 1]) for j in range(8)] for i in range(b + 1, n)]
        for k in range(8):
            s = lax.rsqrt(spread(e[k][k : k + 1]))
            f = jnp.where(sub > k, e[k] * (s * s), 0.0)
            u = [None] * 8
            for j in range(k + 1, 8):
                row = spread(e[j][k : k + 1])
                u[j] = row * s
                e[j] = e[j] - f * row
            prow = spread(p[k : k + 1])
            p = jnp.where(sub == k, prow * s, p - f * prow)
            for ci in cols:
                ci[k] = ci[k] * s
                for j in range(k + 1, 8):
                    ci[j] = ci[j] - ci[k] * u[j]
        for i in range(b + 1, n):
            for k in range(8):
                a[i] = a[i] - cols[i - b - 1][k] * spread(p[k : k + 1])
        a[b] = p
    return jnp.concatenate(a, axis=0)[:, RANK:]


def in_order(c, mine, theirs):
    first = c == 0
    return jnp.where(first, mine, theirs), jnp.where(first, theirs, mine)


def gram_of(c, mine, theirs):
    halves = in_order(c, mine, theirs)
    return jnp.concatenate([p for h in halves for p in (h[:, :RANK], h[:, RANK:])], axis=0)


def put_message(c, left_ref, piece, out_ref):
    own = left_ref[pl.ds(pl.multiple_of(c * PART, PART), PART)]
    wt = dot3(own, piece, 1, 0)
    gram = dot(own, left_ref[...], 1, 1)
    gram = jnp.concatenate([gram[:GRAM], gram[GRAM:]], axis=1)
    for i in range(XY):
        out_ref[i, :PART] = wt
        out_ref[i, PART:] = gram


def half_field(there, base_in, local_in, error_in, base, local, error, sem, out_ref):
    part = HALF // 2
    loads = []
    for i in range(2):
        here = pl.ds(i * part, part)
        rows = pl.ds(pl.multiple_of(there + i * part, part), part)
        for j, (src, dst) in enumerate([(base_in, base), (local_in.at[0], local), (error_in.at[0], error)]):
            load = pltpu.make_async_copy(src.at[rows], dst.at[here], sem.at[i, j])
            load.start()
            loads.append(load)
    for i in range(2):
        here = pl.ds(i * part, part)
        for load in loads[3 * i : 3 * i + 3]:
            load.wait()
        out_ref[here] = base[here] - local[here].astype(F32) + error[here]


def other_half(at_ref, base_in, local_in, error_in, out_ref, base, local, error, sem):
    half_field((1 - at_ref[0]) * HALF, base_in, local_in, error_in, base, local, error, sem, out_ref)


def own_half(at_ref, base_in, local_in, error_in, out_ref, base, local, error, sem):
    half_field(at_ref[0] * HALF, base_in, local_in, error_in, base, local, error, sem, out_ref)


def first_send(low_ref, mine_ref, theirs_ref, query_ref, keep_ref, left_ref, first_ref, second_ref, pair_ref):
    pair_ref[...] = mine_ref[...] + theirs_ref[...]
    low = low_ref[0]
    for h in range(NH):
        slices = [pl.ds(pl.multiple_of((2 * h + l) * SLICE, SLICE), SLICE) for l in (low, 1 - low)]
        keep_ref[h] = pair_ref[:, slices[0]]
        for i, ref in enumerate((first_ref, second_ref)):
            ref[pl.ds(h * PAIRED, PAIRED)] = pair_ref[pl.ds(i * PAIRED, PAIRED), slices[1]]
    left = dot3(pair_ref[...], query_ref[...], 1, 1)
    n = PAIRED // 2
    for i, ref in enumerate((first_ref, second_ref)):
        at = i * PAIRED
        packed = jnp.concatenate([left[at : at + n], left[at + n : at + 2 * n]], axis=1)
        ref[NH * PAIRED :] = packed
        left_ref[i * n : (i + 1) * n] = packed


def fold(high_ref, keep_ref, left_ref, first_ref, second_ref, mine_ref, *out_refs):
    out_ref = out_refs[-1]
    out_refs = (mine_ref,) + out_refs[:-1]
    n = PAIRED // 2
    for i, ref in enumerate((first_ref, second_ref)):
        rows = slice(i * PAIRED, (i + 1) * PAIRED)
        for h in range(NH):
            out_ref[h, rows] = keep_ref[h, rows] + ref[h * PAIRED : (h + 1) * PAIRED]
        packed = left_ref[i * n : (i + 1) * n] + ref[NH * PAIRED :]
        for ref in out_refs:
            ref[HALF + i * n : HALF + (i + 1) * n] = packed
    for k, ref in enumerate(out_refs):
        ref[:HALF] = out_ref[lax.rem(high_ref[0] + k, NH)]


def sum_of_four(refs):
    own, across, one, three = [ref[...] for ref in refs]
    return (own + across) + (one + three)


def mean_over_z(*refs):
    refs[-1][...] = sum_of_four(refs[:-1]) * (1.0 / REPLICAS)


def total_of_four(*refs):
    refs[-1][...] = sum_of_four(refs[:-1])


def first_message(at_ref, mine_ref, theirs_ref, out_ref, piece_ref, left_ref):
    c = at_ref[0]
    halves = in_order(c, mine_ref[...], theirs_ref[...])
    piece = jnp.concatenate([h[:HALF] for h in halves], axis=0)
    n = PAIRED // 2
    left = jnp.concatenate(
        [
            h[at : at + n, lanes]
            for h in halves
            for at in (HALF, HALF + n)
            for lanes in (slice(0, RANK), slice(RANK, 2 * RANK))
        ],
        axis=0,
    )
    piece_ref[...] = piece
    left_ref[...] = left.T
    put_message(c, left_ref, piece, out_ref)


def left_parts(got_ref, piece_ref, out_ref, gram_ref):
    total = add_up(got_ref)
    gram_ref[...] = total[PART:]
    left = dot3(piece_ref[...], total[:PART], 1, 1)
    packed = jnp.concatenate([left[i * LEFT : (i + 1) * LEFT] for i in range(128 // PART)], axis=1)
    out_ref[...] = packed


def factor(at_ref, mine_ref, theirs_ref, out_ref):
    out_ref[...] = inverse_factor(gram_of(at_ref[0], mine_ref[...], theirs_ref[...]))


def add_halves(own_ref, first_ref, second_ref, inv_ref, *out_refs):
    n = first_ref.shape[0]
    for ref in out_refs:
        ref[:n] = own_ref[:n] + first_ref[...]
        ref[n:] = own_ref[n:] + second_ref[...]


def total_of(own_ref, across_ref, one_ref, three_ref, out_ref):
    out_ref[...] = sum_of_four((own_ref, across_ref, one_ref, three_ref))


def next_message(at_ref, mine_ref, theirs_ref, inv_ref, piece_ref, out_ref, left_ref):
    c = at_ref[0]
    first, second = in_order(c, mine_ref[...], theirs_ref[...])
    left = jnp.concatenate(
        [
            jnp.concatenate([h[:, i * PART : (i + 1) * PART] for h in (first, second)], axis=1)
            for i in range(128 // PART)
        ],
        axis=0,
    )
    left_ref[...] = dot(inv_ref[...], left, 1, 1)
    put_message(c, left_ref, piece_ref[...], out_ref)


def right_parts(got_ref, out_ref, gram_ref):
    total = add_up(got_ref)
    gram_ref[...] = total[PART:]
    for i in range(ZC):
        out_ref[i] = total[:PART]


def coefficients(at_ref, mine_ref, theirs_ref, left_ref, base_in, mom_in, coef_ref, base_ref, base, mom, sem):
    loads = [
        pltpu.make_async_copy(src, dst, sem.at[i])
        for i, (src, dst) in enumerate([(base_in, base), (mom_in, mom)])
    ]
    for load in loads:
        load.start()
    inv = inverse_factor(gram_of(at_ref[0], mine_ref[...], theirs_ref[...]))
    basis = dot(inv, left_ref[...], 1, 0)
    high, low = split(dot(basis, inv, 0, 0))
    coef_ref[...] = jnp.concatenate([high, low, high], axis=1)
    for load in loads:
        load.wait()
    base_ref[...] = base[...] - (outer_rate * momentum_decay * momentum_decay) * mom[...]


def finish(at_ref, full_ref, coef_ref, own, other, base, mom_in, base_out, err_out, mom_out,
           mom, nbase, nerr, nmom, in_sem, out_sem):
    c = at_ref[0]
    part = HALF // 2
    count = ROWS // part
    at = [i * part if i < count // 2 else (i - count // 2) * part for i in range(count)]
    here = [pl.ds(i * part, part) for i in range(count)]
    rows = [
        pl.ds(pl.multiple_of((c if i < count // 2 else 1 - c) * HALF + at[i], part), part)
        for i in range(count)
    ]
    loads = [
        pltpu.make_async_copy(mom_in.at[rows[i]], mom.at[here[i]], in_sem.at[i]) for i in range(count)
    ]
    for load in loads:
        load.start()
    wt = jnp.concatenate(
        [jnp.concatenate([full_ref[z * NC + k] for k in range(NC)], axis=0) for z in range(NZ)], axis=1
    )
    high, low = split(wt)
    wt = jnp.concatenate([high, high, low], axis=0)
    stores = []

    def store(j, i, src, dst):
        copy = pltpu.make_async_copy(src.at[here[i]], dst.at[rows[i]], out_sem.at[j, i])
        copy.start()
        stores.append(copy)

    for i in range(count):
        field = own if i < count // 2 else other
        approx = jnp.dot(coef_ref[rows[i]], wt, preferred_element_type=F32)
        nerr[here[i]] = field[pl.ds(at[i], part)] - approx
        store(0, i, nerr, err_out)
        nbase[here[i]] = base[rows[i]] - (outer_rate * (1.0 + momentum_decay)) * approx
        store(1, i, nbase, base_out)
        loads[i].wait()
        nmom[here[i]] = momentum_decay * mom[here[i]] + approx
        store(2, i, nmom, mom_out)
    for copy in stores:
        copy.wait()


def exchange(operand, axes):
    return lax.all_to_all(operand, axes, 0, 0, tiled=True)


def in_hbm(x):
    return pltpu.with_memory_space_constraint(x, pltpu.HBM)


def in_vmem(x):
    return pltpu.with_memory_space_constraint(x, pltpu.VMEM)


def ring(sends, axis):
    return [lax.ppermute(sends[k - 1], axis, [(i, (i + k) % 4) for i in range(4)]) for k in (2, 1, 3)]


def swap(x):
    return lax.ppermute(x, "c", SWAP)


def body(base, local, error, momentum, query):
    c = lax.axis_index("c")
    at = c.astype(jnp.int32)[None]
    low = lax.axis_index("l").astype(jnp.int32)[None]
    buffers = [pltpu.VMEM((HALF, KV), t) for t in (F32, jnp.bfloat16, F32)]
    buffers.append(pltpu.SemaphoreType.DMA((2, 3)))
    half = lambda kernel: call(kernel, shape(HALF, KV), [SMEM] + [HBM] * 3, buffers)(
        at, in_hbm(base), in_hbm(local), in_hbm(error)
    )
    other = half(other_half)
    theirs = swap(other)
    own = half(own_half)
    message = shape(NH * PAIRED + PAIRED // 2, 128)
    keep, left, first, second = call(
        first_send,
        [shape(NH, HALF, SLICE), shape(HALF // 2, 128), message, message],
        [SMEM] + [VMEM] * 3,
        [pltpu.VMEM((HALF, KV), F32)],
    )(low, own, theirs, query.T)
    first = lax.ppermute(first, Z, PAIRS[0])
    second = lax.ppermute(second, Z, PAIRS[1])
    high = lax.axis_index("h").astype(jnp.int32)[None]
    chunk = shape(HALF + HALF // 2, 128)
    mine, *sends = call(fold, [chunk] * NH, [SMEM] + [VMEM] * 4, [pltpu.VMEM((NH, HALF, SLICE), F32)])(
        high, keep, left, first, second
    )
    mean = call(mean_over_z, chunk, [VMEM] * NH)(mine, *ring(sends, "h"))
    send, piece, left = call(
        first_message, [shape(XY, PACK, 128), shape(ROWS, SLICE), shape(RANK, ROWS)], [SMEM] + [VMEM] * 2
    )(at, mean, swap(mean))
    for step in range(1, ITERS):
        send, gram = call(left_parts, [shape(LEFT, 128), shape(GRAM, 128)], [VMEM] * 2)(
            exchange(send, ("x", "y")), piece
        )
        n = LEFT // 2
        pairs = [lax.ppermute(send[i * n : (i + 1) * n], Z, PAIRS[i]) for i in range(2)]
        inv = call(factor, shape(RANK, RANK), [SMEM] + [VMEM] * 2, flops=10**9)(at, gram, swap(gram))
        mine, *sends = call(add_halves, [shape(LEFT, 128)] * NH, [VMEM] * 3 + [HBM])(send, *pairs, inv)
        part = call(total_of, shape(LEFT, 128), [VMEM] * 4)(mine, *ring(sends, "h"))
        send, left = call(
            next_message, [shape(XY, PACK, 128), shape(RANK, ROWS)], [SMEM] + [VMEM] * 4
        )(at, part, swap(part), inv, piece)
    send, gram = call(right_parts, [shape(ZC, PART, 128), shape(GRAM, 128)], [VMEM])(
        exchange(send, ("x", "y"))
    )
    full = exchange(in_vmem(send), Z + ("c",))
    whole = shape(ROWS, KV)
    big = pltpu.VMEM((ROWS, KV), F32)
    coef, partial_base = call(
        coefficients,
        [jax.ShapeDtypeStruct((ROWS, 3 * RANK), jnp.bfloat16), whole],
        [SMEM] + [VMEM] * 3 + [HBM] * 2,
        [big] * 2 + [pltpu.SemaphoreType.DMA((2,))],
        flops=10**9,
    )(at, gram, swap(gram), left, in_hbm(base), in_hbm(momentum))
    new_base, new_error, new_momentum = pl.pallas_call(
        finish,
        out_shape=[whole] * 3,
        in_specs=[SMEM] + [VMEM] * 5 + [HBM],
        out_specs=[HBM] * 3,
        scratch_shapes=[big] * 4 + [pltpu.SemaphoreType.DMA((4,)), pltpu.SemaphoreType.DMA((3, 4))],
        compiler_params=pltpu.CompilerParams(vmem_limit_bytes=16 * 2**20),
    )(at, full, coef, in_vmem(own), in_vmem(other), in_vmem(partial_base), in_hbm(momentum))
    return new_base, new_error[None], new_momentum


def solution(mesh):
    mesh = Mesh(mesh.devices.reshape(NH, 2, NC, NX, NY), ("h", "l", "c", "x", "y"))
    outer, shard = ("h", "l", "c"), ("x", "y")
    in_specs = (
        P(shard, None),
        P(outer, shard, None),
        P(outer, shard, None),
        P(shard, None),
        P(),
    )
    out_specs = (P(shard, None), P(outer, shard, None), P(shard, None))
    return jax.shard_map(body, mesh=mesh, in_specs=in_specs, out_specs=out_specs, check_vma=False)
```

```python
import functools
import jax
import jax.numpy as jnp
from jax import lax
from jax.experimental import pallas as pl
from jax.experimental.pallas import tpu as pltpu
from jax.sharding import Mesh, PartitionSpec as P

ITERS = 2
REPLICAS = 16
RANK = 64
NZ, NC, NX, NY = 8, 2, 4, 4
NH = NZ // 2
Z = ("h", "l")
XY, ZC = NX * NY, NZ * NC
ROWS = 320
HALF = ROWS // 2
KV = 1024
SLICE = KV // NZ
PART = RANK // NC
LEFT = ROWS * PART // 128
GRAM = PART * RANK // 128
PACK = PART + GRAM

momentum_decay = 0.9
outer_rate = 0.7

HI = lax.Precision.HIGHEST
SWAP = [(0, 1), (1, 0)]
PAIRS = (
    [(i, i ^ 1) for i in range(NZ)],
    [(i, (i + 1 if i % 2 else i - 1) % NZ) for i in range(NZ)],
)
PAIRED = HALF // 2
DISTANCES = (0, 2, 1, 3)
F32 = jnp.float32
VMEM = pl.BlockSpec(memory_space=pltpu.VMEM)
SMEM = pl.BlockSpec(memory_space=pltpu.SMEM)
HBM = pl.BlockSpec(memory_space=pltpu.HBM)


def shape(*dims):
    return jax.ShapeDtypeStruct(dims, F32)


def call(kernel, outs, ins, scratch=(), mib=8, flops=10**6):
    return pl.pallas_call(
        kernel,
        out_shape=outs,
        in_specs=ins,
        out_specs=jax.tree.map(lambda _: VMEM, outs),
        scratch_shapes=list(scratch),
        compiler_params=pltpu.CompilerParams(vmem_limit_bytes=mib * 2**20),
        cost_estimate=pl.CostEstimate(flops=flops, bytes_accessed=2**20, transcendentals=0),
    )


def dot(a, b, ca, cb):
    return lax.dot_general(a, b, (((ca,), (cb,)), ((), ())), precision=HI, preferred_element_type=F32)


def split(x):
    high = x.astype(jnp.bfloat16)
    return high, (x - high.astype(F32)).astype(jnp.bfloat16)


def dot3(a, b, ca, cb):
    (ah, al), (bh, bl) = split(a), split(b)
    one = lambda x, y: lax.dot_general(x, y, (((ca,), (cb,)), ((), ())), preferred_element_type=F32)
    return one(ah, bh) + (one(al, bh) + one(ah, bl))


def add_up(ref):
    return functools.reduce(lambda a, b: a + b, [ref[i] for i in range(ref.shape[0])])


def spread(x):
    return jnp.broadcast_to(x, (8, 128))


def inverse_factor(gram):
    n = RANK // 8
    eye = (
        lax.broadcasted_iota(jnp.int32, (RANK, RANK), 0)
        == lax.broadcasted_iota(jnp.int32, (RANK, RANK), 1)
    ).astype(F32)
    full = jnp.concatenate([gram, eye], axis=1)
    a = [full[8 * i : 8 * i + 8] for i in range(n)]
    sub = lax.broadcasted_iota(jnp.int32, (8, 128), 0)
    for b in range(n):
        p = a[b]
        at = 8 * b
        e = [spread(p[:, at + j : at + j + 1]) for j in range(8)]
        cols = [[spread(a[i][:, at + j : at + j + 1]) for j in range(8)] for i in range(b + 1, n)]
        for k in range(8):
            s = lax.rsqrt(spread(e[k][k : k + 1]))
            f = jnp.where(sub > k, e[k] * (s * s), 0.0)
            u = [None] * 8
            for j in range(k + 1, 8):
                row = spread(e[j][k : k + 1])
                u[j] = row * s
                e[j] = e[j] - f * row
            prow = spread(p[k : k + 1])
            p = jnp.where(sub == k, prow * s, p - f * prow)
            for ci in cols:
                ci[k] = ci[k] * s
                for j in range(k + 1, 8):
                    ci[j] = ci[j] - ci[k] * u[j]
        for i in range(b + 1, n):
            for k in range(8):
                a[i] = a[i] - cols[i - b - 1][k] * spread(p[k : k + 1])
        a[b] = p
    return jnp.concatenate(a, axis=0)[:, RANK:]


def in_order(c, mine, theirs):
    first = c == 0
    return jnp.where(first, mine, theirs), jnp.where(first, theirs, mine)


def gram_of(c, mine, theirs):
    halves = in_order(c, mine, theirs)
    return jnp.concatenate([p for h in halves for p in (h[:, :RANK], h[:, RANK:])], axis=0)


def put_message(c, left_ref, piece, out_ref):
    own = left_ref[pl.ds(pl.multiple_of(c * PART, PART), PART)]
    wt = dot3(own, piece, 1, 0)
    gram = dot(own, left_ref[...], 1, 1)
    gram = jnp.concatenate([gram[:GRAM], gram[GRAM:]], axis=1)
    for i in range(XY):
        out_ref[i, :PART] = wt
        out_ref[i, PART:] = gram


def half_field(there, base_in, local_in, error_in, base, local, error, sem, out_ref):
    part = HALF // 2
    loads = []
    for i in range(2):
        here = pl.ds(i * part, part)
        rows = pl.ds(pl.multiple_of(there + i * part, part), part)
        for j, (src, dst) in enumerate([(base_in, base), (local_in.at[0], local), (error_in.at[0], error)]):
            load = pltpu.make_async_copy(src.at[rows], dst.at[here], sem.at[i, j])
            load.start()
            loads.append(load)
    for i in range(2):
        here = pl.ds(i * part, part)
        for load in loads[3 * i : 3 * i + 3]:
            load.wait()
        out_ref[here] = base[here] - local[here].astype(F32) + error[here]


def other_half(at_ref, base_in, local_in, error_in, out_ref, base, local, error, sem):
    half_field((1 - at_ref[0]) * HALF, base_in, local_in, error_in, base, local, error, sem, out_ref)


def own_half(at_ref, base_in, local_in, error_in, out_ref, base, local, error, sem):
    half_field(at_ref[0] * HALF, base_in, local_in, error_in, base, local, error, sem, out_ref)


def first_send(low_ref, mine_ref, theirs_ref, query_ref, keep_ref, left_ref, first_ref, second_ref, pair_ref):
    pair_ref[...] = mine_ref[...] + theirs_ref[...]
    low = low_ref[0]
    for h in range(NH):
        slices = [pl.ds(pl.multiple_of((2 * h + l) * SLICE, SLICE), SLICE) for l in (low, 1 - low)]
        keep_ref[h] = pair_ref[:, slices[0]]
        for i, ref in enumerate((first_ref, second_ref)):
            ref[pl.ds(h * PAIRED, PAIRED)] = pair_ref[pl.ds(i * PAIRED, PAIRED), slices[1]]
    left = dot3(pair_ref[...], query_ref[...], 1, 1)
    n = PAIRED // 2
    for i, ref in enumerate((first_ref, second_ref)):
        at = i * PAIRED
        packed = jnp.concatenate([left[at : at + n], left[at + n : at + 2 * n]], axis=1)
        ref[NH * PAIRED :] = packed
        left_ref[i * n : (i + 1) * n] = packed


def fold(high_ref, keep_ref, left_ref, first_ref, second_ref, mine_ref, *out_refs):
    out_ref = out_refs[-1]
    out_refs = (mine_ref,) + out_refs[:-1]
    n = PAIRED // 2
    for i, ref in enumerate((first_ref, second_ref)):
        rows = slice(i * PAIRED, (i + 1) * PAIRED)
        for h in range(NH):
            out_ref[h, rows] = keep_ref[h, rows] + ref[h * PAIRED : (h + 1) * PAIRED]
        packed = left_ref[i * n : (i + 1) * n] + ref[NH * PAIRED :]
        for ref in out_refs:
            ref[HALF + i * n : HALF + (i + 1) * n] = packed
    for k, ref in enumerate(out_refs):
        ref[:HALF] = out_ref[lax.rem(high_ref[0] + k, NH)]


def sum_of_four(refs):
    own, across, one, three = [ref[...] for ref in refs]
    return (own + across) + (one + three)


def mean_over_z(*refs):
    refs[-1][...] = sum_of_four(refs[:-1]) * (1.0 / REPLICAS)


def total_of_four(*refs):
    refs[-1][...] = sum_of_four(refs[:-1])


def first_message(at_ref, mine_ref, theirs_ref, out_ref, piece_ref, left_ref):
    c = at_ref[0]
    halves = in_order(c, mine_ref[...], theirs_ref[...])
    piece = jnp.concatenate([h[:HALF] for h in halves], axis=0)
    n = PAIRED // 2
    left = jnp.concatenate(
        [
            h[at : at + n, lanes]
            for h in halves
            for at in (HALF, HALF + n)
            for lanes in (slice(0, RANK), slice(RANK, 2 * RANK))
        ],
        axis=0,
    )
    piece_ref[...] = piece
    left_ref[...] = left.T
    put_message(c, left_ref, piece, out_ref)


def left_parts(got_ref, piece_ref, out_ref, gram_ref):
    total = add_up(got_ref)
    gram_ref[...] = total[PART:]
    left = dot3(piece_ref[...], total[:PART], 1, 1)
    packed = jnp.concatenate([left[i * LEFT : (i + 1) * LEFT] for i in range(128 // PART)], axis=1)
    out_ref[...] = packed


def factor(at_ref, mine_ref, theirs_ref, out_ref):
    out_ref[...] = inverse_factor(gram_of(at_ref[0], mine_ref[...], theirs_ref[...]))


def add_halves(own_ref, first_ref, second_ref, inv_ref, *out_refs):
    n = first_ref.shape[0]
    for ref in out_refs:
        ref[:n] = own_ref[:n] + first_ref[...]
        ref[n:] = own_ref[n:] + second_ref[...]


def total_of(own_ref, across_ref, one_ref, three_ref, out_ref):
    out_ref[...] = sum_of_four((own_ref, across_ref, one_ref, three_ref))


def next_message(at_ref, mine_ref, theirs_ref, inv_ref, piece_ref, out_ref, left_ref):
    c = at_ref[0]
    first, second = in_order(c, mine_ref[...], theirs_ref[...])
    left = jnp.concatenate(
        [
            jnp.concatenate([h[:, i * PART : (i + 1) * PART] for h in (first, second)], axis=1)
            for i in range(128 // PART)
        ],
        axis=0,
    )
    left_ref[...] = dot(inv_ref[...], left, 1, 1)
    put_message(c, left_ref, piece_ref[...], out_ref)


def right_parts(got_ref, out_ref, gram_ref):
    total = add_up(got_ref)
    gram_ref[...] = total[PART:]
    out_ref[...] = total[:PART]


def pair_up(own_ref, theirs_ref, *out_refs):
    for ref in out_refs:
        ref[:PART] = own_ref[...]
        ref[PART:] = theirs_ref[...]


def coefficients(at_ref, mine_ref, theirs_ref, left_ref, base_in, mom_in, coef_ref, base_ref, base, mom, sem):
    loads = [
        pltpu.make_async_copy(src, dst, sem.at[i])
        for i, (src, dst) in enumerate([(base_in, base), (mom_in, mom)])
    ]
    for load in loads:
        load.start()
    inv = inverse_factor(gram_of(at_ref[0], mine_ref[...], theirs_ref[...]))
    basis = dot(inv, left_ref[...], 1, 0)
    high, low = split(dot(basis, inv, 0, 0))
    coef_ref[...] = jnp.concatenate([high, low, high], axis=1)
    for load in loads:
        load.wait()
    base_ref[...] = base[...] - (outer_rate * momentum_decay * momentum_decay) * mom[...]


def finish(at_ref, low_ref, high_ref, *refs):
    slices, refs = refs[: 2 * NH], refs[2 * NH :]
    wt_ref = refs[-1]
    for i, ref in enumerate(slices):
        core = at_ref[0] if i < NH else 1 - at_ref[0]
        ranks = pl.ds(pl.multiple_of(core * PART, PART), PART)
        h = lax.rem(high_ref[0] + NH - DISTANCES[i % NH], NH)
        for j in range(2):
            l = low_ref[0] if j == 0 else 1 - low_ref[0]
            wt_ref[2 * h + l, ranks] = ref[j * PART : (j + 1) * PART]
    write_outputs(at_ref, *refs)


def write_outputs(at_ref, coef_ref, own, other, base, mom_in, base_out, err_out, mom_out,
           mom, nbase, nerr, nmom, in_sem, out_sem, wt_ref):
    c = at_ref[0]
    part = HALF // 2
    count = ROWS // part
    at = [i * part if i < count // 2 else (i - count // 2) * part for i in range(count)]
    here = [pl.ds(i * part, part) for i in range(count)]
    rows = [
        pl.ds(pl.multiple_of((c if i < count // 2 else 1 - c) * HALF + at[i], part), part)
        for i in range(count)
    ]
    loads = [
        pltpu.make_async_copy(mom_in.at[rows[i]], mom.at[here[i]], in_sem.at[i]) for i in range(count)
    ]
    for load in loads:
        load.start()
    wt = jnp.concatenate([wt_ref[z] for z in range(NZ)], axis=1)
    high, low = split(wt)
    wt = jnp.concatenate([high, high, low], axis=0)
    stores = []

    def store(j, i, src, dst):
        copy = pltpu.make_async_copy(src.at[here[i]], dst.at[rows[i]], out_sem.at[j, i])
        copy.start()
        stores.append(copy)

    for i in range(count):
        field = own if i < count // 2 else other
        approx = jnp.dot(coef_ref[rows[i]], wt, preferred_element_type=F32)
        nerr[here[i]] = field[pl.ds(at[i], part)] - approx
        store(0, i, nerr, err_out)
        nbase[here[i]] = base[rows[i]] - (outer_rate * (1.0 + momentum_decay)) * approx
        store(1, i, nbase, base_out)
        loads[i].wait()
        nmom[here[i]] = momentum_decay * mom[here[i]] + approx
        store(2, i, nmom, mom_out)
    for copy in stores:
        copy.wait()


def exchange(operand, axes):
    return lax.all_to_all(operand, axes, 0, 0, tiled=True)


def in_hbm(x):
    return pltpu.with_memory_space_constraint(x, pltpu.HBM)


def in_vmem(x):
    return pltpu.with_memory_space_constraint(x, pltpu.VMEM)


def ring(sends, axis):
    return [lax.ppermute(sends[k - 1], axis, [(i, (i + k) % 4) for i in range(4)]) for k in DISTANCES[1:]]


def swap(x):
    return lax.ppermute(x, "c", SWAP)


def body(base, local, error, momentum, query):
    c = lax.axis_index("c")
    at = c.astype(jnp.int32)[None]
    low = lax.axis_index("l").astype(jnp.int32)[None]
    buffers = [pltpu.VMEM((HALF, KV), t) for t in (F32, jnp.bfloat16, F32)]
    buffers.append(pltpu.SemaphoreType.DMA((2, 3)))
    half = lambda kernel: call(kernel, shape(HALF, KV), [SMEM] + [HBM] * 3, buffers)(
        at, in_hbm(base), in_hbm(local), in_hbm(error)
    )
    other = half(other_half)
    theirs = swap(other)
    own = half(own_half)
    message = shape(NH * PAIRED + PAIRED // 2, 128)
    keep, left, first, second = call(
        first_send,
        [shape(NH, HALF, SLICE), shape(HALF // 2, 128), message, message],
        [SMEM] + [VMEM] * 3,
        [pltpu.VMEM((HALF, KV), F32)],
    )(low, own, theirs, query.T)
    first = lax.ppermute(first, Z, PAIRS[0])
    second = lax.ppermute(second, Z, PAIRS[1])
    high = lax.axis_index("h").astype(jnp.int32)[None]
    chunk = shape(HALF + HALF // 2, 128)
    mine, *sends = call(fold, [chunk] * NH, [SMEM] + [VMEM] * 4, [pltpu.VMEM((NH, HALF, SLICE), F32)])(
        high, keep, left, first, second
    )
    mean = call(mean_over_z, chunk, [VMEM] * NH)(mine, *ring(sends, "h"))
    send, piece, left = call(
        first_message, [shape(XY, PACK, 128), shape(ROWS, SLICE), shape(RANK, ROWS)], [SMEM] + [VMEM] * 2
    )(at, mean, swap(mean))
    for step in range(1, ITERS):
        send, gram = call(left_parts, [shape(LEFT, 128), shape(GRAM, 128)], [VMEM] * 2)(
            exchange(send, ("x", "y")), piece
        )
        n = LEFT // 2
        pairs = [lax.ppermute(send[i * n : (i + 1) * n], Z, PAIRS[i]) for i in range(2)]
        inv = call(factor, shape(RANK, RANK), [SMEM] + [VMEM] * 2, flops=10**9)(at, gram, swap(gram))
        mine, *sends = call(add_halves, [shape(LEFT, 128)] * NH, [VMEM] * 3 + [HBM])(send, *pairs, inv)
        part = call(total_of, shape(LEFT, 128), [VMEM] * 4)(mine, *ring(sends, "h"))
        send, left = call(
            next_message, [shape(XY, PACK, 128), shape(RANK, ROWS)], [SMEM] + [VMEM] * 4
        )(at, part, swap(part), inv, piece)
    send, gram = call(right_parts, [shape(PART, 128), shape(GRAM, 128)], [VMEM])(
        exchange(send, ("x", "y"))
    )
    other_parity = lax.ppermute(send, Z, PAIRS[0])
    whole = shape(ROWS, KV)
    big = pltpu.VMEM((ROWS, KV), F32)
    coef, partial_base = call(
        coefficients,
        [jax.ShapeDtypeStruct((ROWS, 3 * RANK), jnp.bfloat16), whole],
        [SMEM] + [VMEM] * 3 + [HBM] * 2,
        [big] * 2 + [pltpu.SemaphoreType.DMA((2,))],
        flops=10**9,
    )(at, gram, swap(gram), left, in_hbm(base), in_hbm(momentum))
    mine, *sends = call(pair_up, [shape(2 * PART, 128)] * NH, [VMEM] * 2)(send, other_parity)
    *got, coef = lax.optimization_barrier((*ring(sends, "h"), coef))
    slices = [mine, *got, swap(mine)] + [swap(x) for x in got]
    new_base, new_error, new_momentum = pl.pallas_call(
        finish,
        out_shape=[whole] * 3,
        in_specs=[SMEM] * 3 + [VMEM] * (2 * NH + 4) + [HBM],
        out_specs=[HBM] * 3,
        scratch_shapes=[big] * 4 + [pltpu.SemaphoreType.DMA((4,)), pltpu.SemaphoreType.DMA((3, 4))]
        + [pltpu.VMEM((NZ, RANK, SLICE), F32)],
        compiler_params=pltpu.CompilerParams(vmem_limit_bytes=16 * 2**20),
    )(at, low, high, *slices, coef, in_vmem(own), in_vmem(other), in_vmem(partial_base), in_hbm(momentum))
    return new_base, new_error[None], new_momentum


def solution(mesh):
    mesh = Mesh(mesh.devices.reshape(NH, 2, NC, NX, NY), ("h", "l", "c", "x", "y"))
    outer, shard = ("h", "l", "c"), ("x", "y")
    in_specs = (
        P(shard, None),
        P(outer, shard, None),
        P(outer, shard, None),
        P(shard, None),
        P(),
    )
    out_specs = (P(shard, None), P(outer, shard, None), P(shard, None))
    return jax.shard_map(body, mesh=mesh, in_specs=in_specs, out_specs=out_specs, check_vma=False)
```

```python
import functools
import jax
import jax.numpy as jnp
from jax import lax
from jax.experimental import pallas as pl
from jax.experimental.pallas import tpu as pltpu
from jax.sharding import Mesh, PartitionSpec as P

ITERS = 2
REPLICAS = 16
RANK = 64
NZ, NC, NX, NY = 8, 2, 4, 4
NH = NZ // 2
Z = ("h", "l")
XY, ZC = NX * NY, NZ * NC
ROWS = 320
HALF = ROWS // 2
KV = 1024
SLICE = KV // NZ
PART = RANK // NC
LEFT = ROWS * PART // 128
GRAM = PART * RANK // 128
PACK = PART + GRAM

momentum_decay = 0.9
outer_rate = 0.7

HI = lax.Precision.HIGHEST
SWAP = [(0, 1), (1, 0)]
PAIRS = (
    [(i, i ^ 1) for i in range(NZ)],
    [(i, (i + 1 if i % 2 else i - 1) % NZ) for i in range(NZ)],
)
PAIRED = HALF // 2
DISTANCES = (0, 2, 1, 3)
F32 = jnp.float32
VMEM = pl.BlockSpec(memory_space=pltpu.VMEM)
SMEM = pl.BlockSpec(memory_space=pltpu.SMEM)
HBM = pl.BlockSpec(memory_space=pltpu.HBM)


def shape(*dims):
    return jax.ShapeDtypeStruct(dims, F32)


def call(kernel, outs, ins, scratch=(), mib=8, flops=10**6):
    return pl.pallas_call(
        kernel,
        out_shape=outs,
        in_specs=ins,
        out_specs=jax.tree.map(lambda _: VMEM, outs),
        scratch_shapes=list(scratch),
        compiler_params=pltpu.CompilerParams(vmem_limit_bytes=mib * 2**20),
        cost_estimate=pl.CostEstimate(flops=flops, bytes_accessed=2**20, transcendentals=0),
    )


def dot(a, b, ca, cb):
    return lax.dot_general(a, b, (((ca,), (cb,)), ((), ())), precision=HI, preferred_element_type=F32)


def split(x):
    high = x.astype(jnp.bfloat16)
    return high, (x - high.astype(F32)).astype(jnp.bfloat16)


def dot3(a, b, ca, cb):
    (ah, al), (bh, bl) = split(a), split(b)
    one = lambda x, y: lax.dot_general(x, y, (((ca,), (cb,)), ((), ())), preferred_element_type=F32)
    return one(ah, bh) + (one(al, bh) + one(ah, bl))


def add_up(ref):
    return functools.reduce(lambda a, b: a + b, [ref[i] for i in range(ref.shape[0])])


def spread(x):
    return jnp.broadcast_to(x, (8, 128))


def inverse_factor(gram):
    n = RANK // 8
    eye = (
        lax.broadcasted_iota(jnp.int32, (RANK, RANK), 0)
        == lax.broadcasted_iota(jnp.int32, (RANK, RANK), 1)
    ).astype(F32)
    full = jnp.concatenate([gram, eye], axis=1)
    a = [full[8 * i : 8 * i + 8] for i in range(n)]
    sub = lax.broadcasted_iota(jnp.int32, (8, 128), 0)
    for b in range(n):
        p = a[b]
        at = 8 * b
        e = [spread(p[:, at + j : at + j + 1]) for j in range(8)]
        cols = [[spread(a[i][:, at + j : at + j + 1]) for j in range(8)] for i in range(b + 1, n)]
        for k in range(8):
            s = lax.rsqrt(spread(e[k][k : k + 1]))
            f = jnp.where(sub > k, e[k] * (s * s), 0.0)
            u = [None] * 8
            for j in range(k + 1, 8):
                row = spread(e[j][k : k + 1])
                u[j] = row * s
                e[j] = e[j] - f * row
            prow = spread(p[k : k + 1])
            p = jnp.where(sub == k, prow * s, p - f * prow)
            for ci in cols:
                ci[k] = ci[k] * s
                for j in range(k + 1, 8):
                    ci[j] = ci[j] - ci[k] * u[j]
        for i in range(b + 1, n):
            for k in range(8):
                a[i] = a[i] - cols[i - b - 1][k] * spread(p[k : k + 1])
        a[b] = p
    return jnp.concatenate(a, axis=0)[:, RANK:]


def in_order(c, mine, theirs):
    first = c == 0
    return jnp.where(first, mine, theirs), jnp.where(first, theirs, mine)


def gram_of(c, mine, theirs):
    halves = in_order(c, mine, theirs)
    return jnp.concatenate([p for h in halves for p in (h[:, :RANK], h[:, RANK:])], axis=0)


def put_message(c, left_ref, piece, out_ref):
    own = left_ref[pl.ds(pl.multiple_of(c * PART, PART), PART)]
    wt = dot3(own, piece, 1, 0)
    gram = dot(own, left_ref[...], 1, 1)
    gram = jnp.concatenate([gram[:GRAM], gram[GRAM:]], axis=1)
    for i in range(XY):
        out_ref[i, :PART] = wt
        out_ref[i, PART:] = gram


def half_field(there, base_in, local_in, error_in, base, local, error, sem, out_ref):
    part = HALF // 2
    loads = []
    for i in range(2):
        here = pl.ds(i * part, part)
        rows = pl.ds(pl.multiple_of(there + i * part, part), part)
        for j, (src, dst) in enumerate([(base_in, base), (local_in.at[0], local), (error_in.at[0], error)]):
            load = pltpu.make_async_copy(src.at[rows], dst.at[here], sem.at[i, j])
            load.start()
            loads.append(load)
    for i in range(2):
        here = pl.ds(i * part, part)
        for load in loads[3 * i : 3 * i + 3]:
            load.wait()
        out_ref[here] = base[here] - local[here].astype(F32) + error[here]


def other_half(at_ref, base_in, local_in, error_in, out_ref, base, local, error, sem):
    half_field((1 - at_ref[0]) * HALF, base_in, local_in, error_in, base, local, error, sem, out_ref)


def own_half(at_ref, base_in, local_in, error_in, out_ref, base, local, error, sem):
    half_field(at_ref[0] * HALF, base_in, local_in, error_in, base, local, error, sem, out_ref)


def first_send(low_ref, mine_ref, theirs_ref, query_ref, keep_ref, left_ref, first_ref, second_ref, pair_ref):
    pair_ref[...] = mine_ref[...] + theirs_ref[...]
    low = low_ref[0]
    for h in range(NH):
        slices = [pl.ds(pl.multiple_of((2 * h + l) * SLICE, SLICE), SLICE) for l in (low, 1 - low)]
        keep_ref[h] = pair_ref[:, slices[0]]
        for i, ref in enumerate((first_ref, second_ref)):
            ref[pl.ds(h * PAIRED, PAIRED)] = pair_ref[pl.ds(i * PAIRED, PAIRED), slices[1]]
    left = dot3(pair_ref[...], query_ref[...], 1, 1)
    n = PAIRED // 2
    for i, ref in enumerate((first_ref, second_ref)):
        at = i * PAIRED
        packed = jnp.concatenate([left[at : at + n], left[at + n : at + 2 * n]], axis=1)
        ref[NH * PAIRED :] = packed
        left_ref[i * n : (i + 1) * n] = packed


def fold(high_ref, keep_ref, left_ref, first_ref, second_ref, mine_ref, *out_refs):
    out_ref = out_refs[-1]
    out_refs = (mine_ref,) + out_refs[:-1]
    n = PAIRED // 2
    for i, ref in enumerate((first_ref, second_ref)):
        rows = slice(i * PAIRED, (i + 1) * PAIRED)
        for h in range(NH):
            out_ref[h, rows] = keep_ref[h, rows] + ref[h * PAIRED : (h + 1) * PAIRED]
        packed = left_ref[i * n : (i + 1) * n] + ref[NH * PAIRED :]
        for ref in out_refs:
            ref[HALF + i * n : HALF + (i + 1) * n] = packed
    for k, ref in enumerate(out_refs):
        ref[:HALF] = out_ref[lax.rem(high_ref[0] + k, NH)]


def sum_of_four(refs):
    own, across, one, three = [ref[...] for ref in refs]
    return (own + across) + (one + three)


def mean_over_z(*refs):
    refs[-1][...] = sum_of_four(refs[:-1]) * (1.0 / REPLICAS)


def total_of_four(*refs):
    refs[-1][...] = sum_of_four(refs[:-1])


def first_message(at_ref, mine_ref, theirs_ref, out_ref, piece_ref, left_ref):
    c = at_ref[0]
    halves = in_order(c, mine_ref[...], theirs_ref[...])
    piece = jnp.concatenate([h[:HALF] for h in halves], axis=0)
    n = PAIRED // 2
    left = jnp.concatenate(
        [
            h[at : at + n, lanes]
            for h in halves
            for at in (HALF, HALF + n)
            for lanes in (slice(0, RANK), slice(RANK, 2 * RANK))
        ],
        axis=0,
    )
    piece_ref[...] = piece
    left_ref[...] = left.T
    put_message(c, left_ref, piece, out_ref)


def left_parts(got_ref, piece_ref, out_ref, gram_ref):
    total = add_up(got_ref)
    gram_ref[...] = total[PART:]
    left = dot3(piece_ref[...], total[:PART], 1, 1)
    packed = jnp.concatenate([left[i * LEFT : (i + 1) * LEFT] for i in range(128 // PART)], axis=1)
    out_ref[...] = packed


def factor(at_ref, mine_ref, theirs_ref, out_ref):
    out_ref[...] = inverse_factor(gram_of(at_ref[0], mine_ref[...], theirs_ref[...]))


def add_halves(own_ref, first_ref, second_ref, inv_ref, *out_refs):
    n = first_ref.shape[0]
    for ref in out_refs:
        ref[:n] = own_ref[:n] + first_ref[...]
        ref[n:] = own_ref[n:] + second_ref[...]


def total_of(own_ref, across_ref, one_ref, three_ref, out_ref):
    out_ref[...] = sum_of_four((own_ref, across_ref, one_ref, three_ref))


def next_message(at_ref, mine_ref, theirs_ref, inv_ref, piece_ref, out_ref, left_ref):
    c = at_ref[0]
    first, second = in_order(c, mine_ref[...], theirs_ref[...])
    left = jnp.concatenate(
        [
            jnp.concatenate([h[:, i * PART : (i + 1) * PART] for h in (first, second)], axis=1)
            for i in range(128 // PART)
        ],
        axis=0,
    )
    left_ref[...] = dot(inv_ref[...], left, 1, 1)
    put_message(c, left_ref, piece_ref[...], out_ref)


def right_parts(got_ref, out_ref, gram_ref):
    total = add_up(got_ref)
    gram_ref[...] = total[PART:]
    out_ref[...] = total[:PART]


def pair_up(own_ref, theirs_ref, *out_refs):
    for ref in out_refs:
        ref[:PART] = own_ref[...]
        ref[PART:] = theirs_ref[...]


def join(*refs):
    n = 2 * PART
    for i, ref in enumerate(refs[:-1]):
        refs[-1][i * n : (i + 1) * n] = ref[...]


def coefficients(at_ref, mine_ref, theirs_ref, left_ref, base_in, mom_in, coef_ref, base_ref, base, mom, sem):
    loads = [
        pltpu.make_async_copy(src, dst, sem.at[i])
        for i, (src, dst) in enumerate([(base_in, base), (mom_in, mom)])
    ]
    for load in loads:
        load.start()
    inv = inverse_factor(gram_of(at_ref[0], mine_ref[...], theirs_ref[...]))
    basis = dot(inv, left_ref[...], 1, 0)
    high, low = split(dot(basis, inv, 0, 0))
    coef_ref[...] = jnp.concatenate([high, low, high], axis=1)
    for load in loads:
        load.wait()
    base_ref[...] = base[...] - (outer_rate * momentum_decay * momentum_decay) * mom[...]


def finish(at_ref, low_ref, high_ref, *refs):
    n = 2 * PART
    slices, joined, refs = refs[: NH + 1], refs[NH + 1], refs[NH + 2 :]
    slices += tuple(joined.at[i * n : (i + 1) * n] for i in range(NH - 1))
    wt_ref = refs[-1]
    for i, ref in enumerate(slices):
        core = at_ref[0] if i < NH else 1 - at_ref[0]
        ranks = pl.ds(pl.multiple_of(core * PART, PART), PART)
        h = lax.rem(high_ref[0] + NH - DISTANCES[i % NH], NH)
        for j in range(2):
            l = low_ref[0] if j == 0 else 1 - low_ref[0]
            wt_ref[2 * h + l, ranks] = ref[j * PART : (j + 1) * PART]
    write_outputs(at_ref, *refs)


def write_outputs(at_ref, coef_ref, own, other, base, mom_in, base_out, err_out, mom_out,
           mom, nbase, nerr, nmom, in_sem, out_sem, wt_ref):
    c = at_ref[0]
    part = HALF // 2
    count = ROWS // part
    at = [i * part if i < count // 2 else (i - count // 2) * part for i in range(count)]
    here = [pl.ds(i * part, part) for i in range(count)]
    rows = [
        pl.ds(pl.multiple_of((c if i < count // 2 else 1 - c) * HALF + at[i], part), part)
        for i in range(count)
    ]
    loads = [
        pltpu.make_async_copy(mom_in.at[rows[i]], mom.at[here[i]], in_sem.at[i]) for i in range(count)
    ]
    for load in loads:
        load.start()
    wt = jnp.concatenate([wt_ref[z] for z in range(NZ)], axis=1)
    high, low = split(wt)
    wt = jnp.concatenate([high, high, low], axis=0)
    stores = []

    def store(j, i, src, dst):
        copy = pltpu.make_async_copy(src.at[here[i]], dst.at[rows[i]], out_sem.at[j, i])
        copy.start()
        stores.append(copy)

    for i in range(count):
        field = own if i < count // 2 else other
        approx = jnp.dot(coef_ref[rows[i]], wt, preferred_element_type=F32)
        nerr[here[i]] = field[pl.ds(at[i], part)] - approx
        store(0, i, nerr, err_out)
        nbase[here[i]] = base[rows[i]] - (outer_rate * (1.0 + momentum_decay)) * approx
        store(1, i, nbase, base_out)
        loads[i].wait()
        nmom[here[i]] = momentum_decay * mom[here[i]] + approx
        store(2, i, nmom, mom_out)
    for copy in stores:
        copy.wait()


def exchange(operand, axes):
    return lax.all_to_all(operand, axes, 0, 0, tiled=True)


def in_hbm(x):
    return pltpu.with_memory_space_constraint(x, pltpu.HBM)


def in_vmem(x):
    return pltpu.with_memory_space_constraint(x, pltpu.VMEM)


def ring(sends, axis):
    return [lax.ppermute(sends[k - 1], axis, [(i, (i + k) % 4) for i in range(4)]) for k in DISTANCES[1:]]


def swap(x):
    return lax.ppermute(x, "c", SWAP)


def body(base, local, error, momentum, query):
    c = lax.axis_index("c")
    at = c.astype(jnp.int32)[None]
    low = lax.axis_index("l").astype(jnp.int32)[None]
    buffers = [pltpu.VMEM((HALF, KV), t) for t in (F32, jnp.bfloat16, F32)]
    buffers.append(pltpu.SemaphoreType.DMA((2, 3)))
    half = lambda kernel: call(kernel, shape(HALF, KV), [SMEM] + [HBM] * 3, buffers)(
        at, in_hbm(base), in_hbm(local), in_hbm(error)
    )
    other = half(other_half)
    theirs = swap(other)
    own = half(own_half)
    message = shape(NH * PAIRED + PAIRED // 2, 128)
    keep, left, first, second = call(
        first_send,
        [shape(NH, HALF, SLICE), shape(HALF // 2, 128), message, message],
        [SMEM] + [VMEM] * 3,
        [pltpu.VMEM((HALF, KV), F32)],
    )(low, own, theirs, query.T)
    first = lax.ppermute(first, Z, PAIRS[0])
    second = lax.ppermute(second, Z, PAIRS[1])
    high = lax.axis_index("h").astype(jnp.int32)[None]
    chunk = shape(HALF + HALF // 2, 128)
    mine, *sends = call(fold, [chunk] * NH, [SMEM] + [VMEM] * 4, [pltpu.VMEM((NH, HALF, SLICE), F32)])(
        high, keep, left, first, second
    )
    mean = call(mean_over_z, chunk, [VMEM] * NH)(mine, *ring(sends, "h"))
    send, piece, left = call(
        first_message, [shape(XY, PACK, 128), shape(ROWS, SLICE), shape(RANK, ROWS)], [SMEM] + [VMEM] * 2
    )(at, mean, swap(mean))
    for step in range(1, ITERS):
        send, gram = call(left_parts, [shape(LEFT, 128), shape(GRAM, 128)], [VMEM] * 2)(
            exchange(send, ("x", "y")), piece
        )
        n = LEFT // 2
        pairs = [lax.ppermute(send[i * n : (i + 1) * n], Z, PAIRS[i]) for i in range(2)]
        inv = call(factor, shape(RANK, RANK), [SMEM] + [VMEM] * 2, flops=10**9)(at, gram, swap(gram))
        mine, *sends = call(add_halves, [shape(LEFT, 128)] * NH, [VMEM] * 3 + [HBM])(send, *pairs, inv)
        part = call(total_of, shape(LEFT, 128), [VMEM] * 4)(mine, *ring(sends, "h"))
        send, left = call(
            next_message, [shape(XY, PACK, 128), shape(RANK, ROWS)], [SMEM] + [VMEM] * 4
        )(at, part, swap(part), inv, piece)
    send, gram = call(right_parts, [shape(PART, 128), shape(GRAM, 128)], [VMEM])(
        exchange(send, ("x", "y"))
    )
    other_parity = lax.ppermute(send, Z, PAIRS[0])
    whole = shape(ROWS, KV)
    big = pltpu.VMEM((ROWS, KV), F32)
    coef, partial_base = call(
        coefficients,
        [jax.ShapeDtypeStruct((ROWS, 3 * RANK), jnp.bfloat16), whole],
        [SMEM] + [VMEM] * 3 + [HBM] * 2,
        [big] * 2 + [pltpu.SemaphoreType.DMA((2,))],
        flops=10**9,
    )(at, gram, swap(gram), left, in_hbm(base), in_hbm(momentum))
    mine, *sends = call(pair_up, [shape(2 * PART, 128)] * NH, [VMEM] * 2)(send, other_parity)
    *got, coef = lax.optimization_barrier((*ring(sends, "h"), coef))
    joined = call(join, shape(2 * PART * (NH - 1), 128), [VMEM] * (NH - 1))(*got)
    slices = [mine, *got, swap(mine), swap(joined)]
    new_base, new_error, new_momentum = pl.pallas_call(
        finish,
        out_shape=[whole] * 3,
        in_specs=[SMEM] * 3 + [VMEM] * (NH + 6) + [HBM],
        out_specs=[HBM] * 3,
        scratch_shapes=[big] * 4 + [pltpu.SemaphoreType.DMA((4,)), pltpu.SemaphoreType.DMA((3, 4))]
        + [pltpu.VMEM((NZ, RANK, SLICE), F32)],
        compiler_params=pltpu.CompilerParams(vmem_limit_bytes=16 * 2**20),
    )(at, low, high, *slices, coef, in_vmem(own), in_vmem(other), in_vmem(partial_base), in_hbm(momentum))
    return new_base, new_error[None], new_momentum


def solution(mesh):
    mesh = Mesh(mesh.devices.reshape(NH, 2, NC, NX, NY), ("h", "l", "c", "x", "y"))
    outer, shard = ("h", "l", "c"), ("x", "y")
    in_specs = (
        P(shard, None),
        P(outer, shard, None),
        P(outer, shard, None),
        P(shard, None),
        P(),
    )
    out_specs = (P(shard, None), P(outer, shard, None), P(shard, None))
    return jax.shard_map(body, mesh=mesh, in_specs=in_specs, out_specs=out_specs, check_vma=False)
```

```python
import functools
import jax
import jax.numpy as jnp
from jax import lax
from jax.experimental import pallas as pl
from jax.experimental.pallas import tpu as pltpu
from jax.sharding import Mesh, PartitionSpec as P

ITERS = 2
REPLICAS = 16
RANK = 64
NZ, NC, NX, NY = 8, 2, 4, 4
NH = NZ // 2
Z = ("h", "l")
XY, ZC = NX * NY, NZ * NC
ROWS = 320
HALF = ROWS // 2
KV = 1024
SLICE = KV // NZ
PART = RANK // NC
LEFT = ROWS * PART // 128
GRAM = PART * RANK // 128
PACK = PART + GRAM

momentum_decay = 0.9
outer_rate = 0.7

HI = lax.Precision.HIGHEST
SWAP = [(0, 1), (1, 0)]
PAIRS = (
    [(i, i ^ 1) for i in range(NZ)],
    [(i, (i + 1 if i % 2 else i - 1) % NZ) for i in range(NZ)],
)
PAIRED = HALF // 2
DISTANCES = (0, 2, 1, 3)
F32 = jnp.float32
VMEM = pl.BlockSpec(memory_space=pltpu.VMEM)
SMEM = pl.BlockSpec(memory_space=pltpu.SMEM)
HBM = pl.BlockSpec(memory_space=pltpu.HBM)


def shape(*dims):
    return jax.ShapeDtypeStruct(dims, F32)


def call(kernel, outs, ins, scratch=(), mib=8, flops=10**6):
    return pl.pallas_call(
        kernel,
        out_shape=outs,
        in_specs=ins,
        out_specs=jax.tree.map(lambda _: VMEM, outs),
        scratch_shapes=list(scratch),
        compiler_params=pltpu.CompilerParams(vmem_limit_bytes=mib * 2**20),
        cost_estimate=pl.CostEstimate(flops=flops, bytes_accessed=2**20, transcendentals=0),
    )


def dot(a, b, ca, cb):
    return lax.dot_general(a, b, (((ca,), (cb,)), ((), ())), precision=HI, preferred_element_type=F32)


def split(x):
    high = x.astype(jnp.bfloat16)
    return high, (x - high.astype(F32)).astype(jnp.bfloat16)


def dot3(a, b, ca, cb):
    (ah, al), (bh, bl) = split(a), split(b)
    one = lambda x, y: lax.dot_general(x, y, (((ca,), (cb,)), ((), ())), preferred_element_type=F32)
    return one(ah, bh) + (one(al, bh) + one(ah, bl))


def add_up(ref):
    return functools.reduce(lambda a, b: a + b, [ref[i] for i in range(ref.shape[0])])


def spread(x):
    return jnp.broadcast_to(x, (8, 128))


def inverse_factor(gram):
    n = RANK // 8
    eye = (
        lax.broadcasted_iota(jnp.int32, (RANK, RANK), 0)
        == lax.broadcasted_iota(jnp.int32, (RANK, RANK), 1)
    ).astype(F32)
    full = jnp.concatenate([gram, eye], axis=1)
    a = [full[8 * i : 8 * i + 8] for i in range(n)]
    sub = lax.broadcasted_iota(jnp.int32, (8, 128), 0)
    for b in range(n):
        p = a[b]
        at = 8 * b
        e = [spread(p[:, at + j : at + j + 1]) for j in range(8)]
        cols = [[spread(a[i][:, at + j : at + j + 1]) for j in range(8)] for i in range(b + 1, n)]
        for k in range(8):
            s = lax.rsqrt(spread(e[k][k : k + 1]))
            f = jnp.where(sub > k, e[k] * (s * s), 0.0)
            u = [None] * 8
            for j in range(k + 1, 8):
                row = spread(e[j][k : k + 1])
                u[j] = row * s
                e[j] = e[j] - f * row
            prow = spread(p[k : k + 1])
            p = jnp.where(sub == k, prow * s, p - f * prow)
            for ci in cols:
                ci[k] = ci[k] * s
                for j in range(k + 1, 8):
                    ci[j] = ci[j] - ci[k] * u[j]
        for i in range(b + 1, n):
            for k in range(8):
                a[i] = a[i] - cols[i - b - 1][k] * spread(p[k : k + 1])
        a[b] = p
    return jnp.concatenate(a, axis=0)[:, RANK:]


def in_order(c, mine, theirs):
    first = c == 0
    return jnp.where(first, mine, theirs), jnp.where(first, theirs, mine)


def gram_of(c, mine, theirs):
    halves = in_order(c, mine, theirs)
    return jnp.concatenate([p for h in halves for p in (h[:, :RANK], h[:, RANK:])], axis=0)


def put_message(c, left_ref, piece, out_ref):
    own = left_ref[pl.ds(pl.multiple_of(c * PART, PART), PART)]
    wt = dot3(own, piece, 1, 0)
    gram = dot(own, left_ref[...], 1, 1)
    gram = jnp.concatenate([gram[:GRAM], gram[GRAM:]], axis=1)
    for i in range(XY):
        out_ref[i, :PART] = wt
        out_ref[i, PART:] = gram


def half_field(there, base_in, local_in, error_in, base, local, error, sem, out_ref):
    part = HALF // 2
    loads = []
    for i in range(2):
        here = pl.ds(i * part, part)
        rows = pl.ds(pl.multiple_of(there + i * part, part), part)
        for j, (src, dst) in enumerate([(base_in, base), (local_in.at[0], local), (error_in.at[0], error)]):
            load = pltpu.make_async_copy(src.at[rows], dst.at[here], sem.at[i, j])
            load.start()
            loads.append(load)
    for i in range(2):
        here = pl.ds(i * part, part)
        for load in loads[3 * i : 3 * i + 3]:
            load.wait()
        out_ref[here] = base[here] - local[here].astype(F32) + error[here]


def other_half(at_ref, base_in, local_in, error_in, out_ref, base, local, error, sem):
    half_field((1 - at_ref[0]) * HALF, base_in, local_in, error_in, base, local, error, sem, out_ref)


def own_half(at_ref, base_in, local_in, error_in, out_ref, base, local, error, sem):
    half_field(at_ref[0] * HALF, base_in, local_in, error_in, base, local, error, sem, out_ref)


def first_send(low_ref, mine_ref, theirs_ref, query_ref, keep_ref, left_ref, first_ref, second_ref, pair_ref):
    pair_ref[...] = mine_ref[...] + theirs_ref[...]
    low = low_ref[0]
    for h in range(NH):
        slices = [pl.ds(pl.multiple_of((2 * h + l) * SLICE, SLICE), SLICE) for l in (low, 1 - low)]
        keep_ref[h] = pair_ref[:, slices[0]]
        for i, ref in enumerate((first_ref, second_ref)):
            ref[pl.ds(h * PAIRED, PAIRED)] = pair_ref[pl.ds(i * PAIRED, PAIRED), slices[1]]
    left = dot3(pair_ref[...], query_ref[...], 1, 1)
    n = PAIRED // 2
    for i, ref in enumerate((first_ref, second_ref)):
        at = i * PAIRED
        packed = jnp.concatenate([left[at : at + n], left[at + n : at + 2 * n]], axis=1)
        ref[NH * PAIRED :] = packed
        left_ref[i * n : (i + 1) * n] = packed


def fold(high_ref, keep_ref, left_ref, first_ref, second_ref, mine_ref, *out_refs):
    out_ref = out_refs[-1]
    out_refs = (mine_ref,) + out_refs[:-1]
    n = PAIRED // 2
    for i, ref in enumerate((first_ref, second_ref)):
        rows = slice(i * PAIRED, (i + 1) * PAIRED)
        for h in range(NH):
            out_ref[h, rows] = keep_ref[h, rows] + ref[h * PAIRED : (h + 1) * PAIRED]
        packed = left_ref[i * n : (i + 1) * n] + ref[NH * PAIRED :]
        for ref in out_refs:
            ref[HALF + i * n : HALF + (i + 1) * n] = packed
    for k, ref in enumerate(out_refs):
        ref[:HALF] = out_ref[lax.rem(high_ref[0] + k, NH)]


def sum_of_four(refs):
    own, across, one, three = [ref[...] for ref in refs]
    return (own + across) + (one + three)


def mean_over_z(*refs):
    refs[-1][...] = sum_of_four(refs[:-1]) * (1.0 / REPLICAS)


def total_of_four(*refs):
    refs[-1][...] = sum_of_four(refs[:-1])


def first_message(at_ref, mine_ref, theirs_ref, out_ref, piece_ref, left_ref):
    c = at_ref[0]
    halves = in_order(c, mine_ref[...], theirs_ref[...])
    piece = jnp.concatenate([h[:HALF] for h in halves], axis=0)
    n = PAIRED // 2
    left = jnp.concatenate(
        [
            h[at : at + n, lanes]
            for h in halves
            for at in (HALF, HALF + n)
            for lanes in (slice(0, RANK), slice(RANK, 2 * RANK))
        ],
        axis=0,
    )
    piece_ref[...] = piece
    left_ref[...] = left.T
    put_message(c, left_ref, piece, out_ref)


def left_parts(got_ref, piece_ref, out_ref, gram_ref):
    total = add_up(got_ref)
    gram_ref[...] = total[PART:]
    left = dot3(piece_ref[...], total[:PART], 1, 1)
    packed = jnp.concatenate([left[i * LEFT : (i + 1) * LEFT] for i in range(128 // PART)], axis=1)
    out_ref[...] = packed


def factor(at_ref, mine_ref, theirs_ref, out_ref):
    out_ref[...] = inverse_factor(gram_of(at_ref[0], mine_ref[...], theirs_ref[...]))


def add_halves(own_ref, first_ref, second_ref, inv_ref, *out_refs):
    n = first_ref.shape[0]
    for ref in out_refs:
        ref[:n] = own_ref[:n] + first_ref[...]
        ref[n:] = own_ref[n:] + second_ref[...]


def total_of(own_ref, across_ref, one_ref, three_ref, out_ref):
    out_ref[...] = sum_of_four((own_ref, across_ref, one_ref, three_ref))


def next_message(at_ref, mine_ref, theirs_ref, inv_ref, piece_ref, out_ref, left_ref):
    c = at_ref[0]
    first, second = in_order(c, mine_ref[...], theirs_ref[...])
    left = jnp.concatenate(
        [
            jnp.concatenate([h[:, i * PART : (i + 1) * PART] for h in (first, second)], axis=1)
            for i in range(128 // PART)
        ],
        axis=0,
    )
    left_ref[...] = dot(inv_ref[...], left, 1, 1)
    put_message(c, left_ref, piece_ref[...], out_ref)


def right_parts(got_ref, out_ref, gram_ref):
    total = add_up(got_ref)
    gram_ref[...] = total[PART:]
    out_ref[...] = total[:PART]


def pair_up(own_ref, theirs_ref, *out_refs):
    for ref in out_refs:
        ref[:PART] = own_ref[...]
        ref[PART:] = theirs_ref[...]


def join(*refs):
    n = 2 * PART
    for i, ref in enumerate(refs[:-1]):
        refs[-1][i * n : (i + 1) * n] = ref[...]


def coefficients(at_ref, mine_ref, theirs_ref, left_ref, base_in, mom_in, coef_ref, base_ref, base, mom, sem):
    loads = [
        pltpu.make_async_copy(src, dst, sem.at[i])
        for i, (src, dst) in enumerate([(base_in, base), (mom_in, mom)])
    ]
    for load in loads:
        load.start()
    inv = inverse_factor(gram_of(at_ref[0], mine_ref[...], theirs_ref[...]))
    basis = dot(inv, left_ref[...], 1, 0)
    high, low = split(dot(basis, inv, 0, 0))
    coef_ref[...] = jnp.concatenate([high, low, high], axis=1)
    for load in loads:
        load.wait()
    base_ref[...] = base[...] - (outer_rate * momentum_decay * momentum_decay) * mom[...]


def finish(at_ref, low_ref, high_ref, *refs):
    n = 2 * PART
    slices, joined, refs = refs[: NH + 1], refs[NH + 1], refs[NH + 2 :]
    slices += tuple(joined.at[i * n : (i + 1) * n] for i in range(NH - 1))
    wt_ref = refs[-1]
    for i, ref in enumerate(slices):
        core = at_ref[0] if i < NH else 1 - at_ref[0]
        ranks = pl.ds(pl.multiple_of(core * PART, PART), PART)
        h = lax.rem(high_ref[0] + NH - DISTANCES[i % NH], NH)
        for j in range(2):
            l = low_ref[0] if j == 0 else 1 - low_ref[0]
            wt_ref[2 * h + l, ranks] = ref[j * PART : (j + 1) * PART]
    write_outputs(at_ref, *refs)


def write_outputs(at_ref, coef_ref, own, other, base, mom_in, base_out, err_out, mom_out,
           mom, nbase, nerr, nmom, in_sem, out_sem, wt_ref):
    c = at_ref[0]
    part = HALF // 5
    count = ROWS // part
    at = [i * part if i < count // 2 else (i - count // 2) * part for i in range(count)]
    here = [pl.ds(i * part, part) for i in range(count)]
    rows = [
        pl.ds(pl.multiple_of((c if i < count // 2 else 1 - c) * HALF + at[i], part), part)
        for i in range(count)
    ]
    loads = [
        pltpu.make_async_copy(mom_in.at[rows[i]], mom.at[here[i]], in_sem.at[i]) for i in range(count)
    ]
    for load in loads:
        load.start()
    wt = jnp.concatenate([wt_ref[z] for z in range(NZ)], axis=1)
    high, low = split(wt)
    wt = jnp.concatenate([high, high, low], axis=0)
    stores = []

    def store(j, i, src, dst):
        copy = pltpu.make_async_copy(src.at[here[i]], dst.at[rows[i]], out_sem.at[j, i])
        copy.start()
        stores.append(copy)

    for i in range(count):
        field = own if i < count // 2 else other
        approx = jnp.dot(coef_ref[rows[i]], wt, preferred_element_type=F32)
        nerr[here[i]] = field[pl.ds(at[i], part)] - approx
        store(0, i, nerr, err_out)
        nbase[here[i]] = base[rows[i]] - (outer_rate * (1.0 + momentum_decay)) * approx
        store(1, i, nbase, base_out)
        loads[i].wait()
        nmom[here[i]] = momentum_decay * mom[here[i]] + approx
        store(2, i, nmom, mom_out)
    for copy in stores:
        copy.wait()


def exchange(operand, axes):
    return lax.all_to_all(operand, axes, 0, 0, tiled=True)


def in_hbm(x):
    return pltpu.with_memory_space_constraint(x, pltpu.HBM)


def in_vmem(x):
    return pltpu.with_memory_space_constraint(x, pltpu.VMEM)


def ring(sends, axis):
    return [lax.ppermute(sends[k - 1], axis, [(i, (i + k) % 4) for i in range(4)]) for k in DISTANCES[1:]]


def swap(x):
    return lax.ppermute(x, "c", SWAP)


def body(base, local, error, momentum, query):
    c = lax.axis_index("c")
    at = c.astype(jnp.int32)[None]
    low = lax.axis_index("l").astype(jnp.int32)[None]
    buffers = [pltpu.VMEM((HALF, KV), t) for t in (F32, jnp.bfloat16, F32)]
    buffers.append(pltpu.SemaphoreType.DMA((2, 3)))
    half = lambda kernel: call(kernel, shape(HALF, KV), [SMEM] + [HBM] * 3, buffers)(
        at, in_hbm(base), in_hbm(local), in_hbm(error)
    )
    other = half(other_half)
    theirs = swap(other)
    own = half(own_half)
    message = shape(NH * PAIRED + PAIRED // 2, 128)
    keep, left, first, second = call(
        first_send,
        [shape(NH, HALF, SLICE), shape(HALF // 2, 128), message, message],
        [SMEM] + [VMEM] * 3,
        [pltpu.VMEM((HALF, KV), F32)],
    )(low, own, theirs, query.T)
    first = lax.ppermute(first, Z, PAIRS[0])
    second = lax.ppermute(second, Z, PAIRS[1])
    high = lax.axis_index("h").astype(jnp.int32)[None]
    chunk = shape(HALF + HALF // 2, 128)
    mine, *sends = call(fold, [chunk] * NH, [SMEM] + [VMEM] * 4, [pltpu.VMEM((NH, HALF, SLICE), F32)])(
        high, keep, left, first, second
    )
    mean = call(mean_over_z, chunk, [VMEM] * NH)(mine, *ring(sends, "h"))
    send, piece, left = call(
        first_message, [shape(XY, PACK, 128), shape(ROWS, SLICE), shape(RANK, ROWS)], [SMEM] + [VMEM] * 2
    )(at, mean, swap(mean))
    for step in range(1, ITERS):
        send, gram = call(left_parts, [shape(LEFT, 128), shape(GRAM, 128)], [VMEM] * 2)(
            exchange(send, ("x", "y")), piece
        )
        n = LEFT // 2
        pairs = [lax.ppermute(send[i * n : (i + 1) * n], Z, PAIRS[i]) for i in range(2)]
        inv = call(factor, shape(RANK, RANK), [SMEM] + [VMEM] * 2, flops=10**9)(at, gram, swap(gram))
        mine, *sends = call(add_halves, [shape(LEFT, 128)] * NH, [VMEM] * 3 + [HBM])(send, *pairs, inv)
        part = call(total_of, shape(LEFT, 128), [VMEM] * 4)(mine, *ring(sends, "h"))
        send, left = call(
            next_message, [shape(XY, PACK, 128), shape(RANK, ROWS)], [SMEM] + [VMEM] * 4
        )(at, part, swap(part), inv, piece)
    send, gram = call(right_parts, [shape(PART, 128), shape(GRAM, 128)], [VMEM])(
        exchange(send, ("x", "y"))
    )
    other_parity = lax.ppermute(send, Z, PAIRS[0])
    whole = shape(ROWS, KV)
    big = pltpu.VMEM((ROWS, KV), F32)
    coef, partial_base = call(
        coefficients,
        [jax.ShapeDtypeStruct((ROWS, 3 * RANK), jnp.bfloat16), whole],
        [SMEM] + [VMEM] * 3 + [HBM] * 2,
        [big] * 2 + [pltpu.SemaphoreType.DMA((2,))],
        flops=10**9,
    )(at, gram, swap(gram), left, in_hbm(base), in_hbm(momentum))
    mine, *sends = call(pair_up, [shape(2 * PART, 128)] * NH, [VMEM] * 2)(send, other_parity)
    *got, coef = lax.optimization_barrier((*ring(sends, "h"), coef))
    joined = call(join, shape(2 * PART * (NH - 1), 128), [VMEM] * (NH - 1))(*got)
    slices = [mine, *got, swap(mine), swap(joined)]
    new_base, new_error, new_momentum = pl.pallas_call(
        finish,
        out_shape=[whole] * 3,
        in_specs=[SMEM] * 3 + [VMEM] * (NH + 6) + [HBM],
        out_specs=[HBM] * 3,
        scratch_shapes=[big] * 4 + [pltpu.SemaphoreType.DMA((10,)), pltpu.SemaphoreType.DMA((3, 10))]
        + [pltpu.VMEM((NZ, RANK, SLICE), F32)],
        compiler_params=pltpu.CompilerParams(vmem_limit_bytes=16 * 2**20),
    )(at, low, high, *slices, coef, in_vmem(own), in_vmem(other), in_vmem(partial_base), in_hbm(momentum))
    return new_base, new_error[None], new_momentum


def solution(mesh):
    mesh = Mesh(mesh.devices.reshape(NH, 2, NC, NX, NY), ("h", "l", "c", "x", "y"))
    outer, shard = ("h", "l", "c"), ("x", "y")
    in_specs = (
        P(shard, None),
        P(outer, shard, None),
        P(outer, shard, None),
        P(shard, None),
        P(),
    )
    out_specs = (P(shard, None), P(outer, shard, None), P(shard, None))
    return jax.shard_map(body, mesh=mesh, in_specs=in_specs, out_specs=out_specs, check_vma=False)
```
